32 devices in a mesh: tm: 4 (over z), state: 4 (over y, x), outputs: 2 (over core).
Axes of the slice: x: 2, y: 2, z: 4, core: 2. Of those that a mesh axis runs over, the one named last changes fastest.
Arguments:
- observations: float32 [48, 512], P('tm', 'outputs'), may hold values from -6 to 6
- observed: int32 [48, 512], P('tm', 'outputs'), may hold values 0 or 1
- loadings: float32 [48, 512, 512], P('tm', 'outputs'), may hold values from -0.25 to 0.25
- noise_precision: float32 [512], P('outputs'), may hold values from 0.25 to 1
- blend_matrix: float32 [512, 512], replicated, may hold values from -0.02 to 0.1, as said below
- latent_rates: float32 [4], replicated, may hold values from 0.03 to 1
- pair_latent: int32 [256], replicated, may hold values from 0 to 3
- initial_mean: float32 [512], replicated, may hold values from -6 to 6
Outputs:
- states: float32 [48, 512], P('tm', 'state')
- predicted: float32 [48, 512], P('tm', 'outputs')
The draws below stay inside these ranges and needn't reach their ends.
Inputs may be any that keep to these rules, and one draw needn't show every extreme that they name: `blend_matrix`: symmetric, positive definite.
All inputs are finite; a program needn't handle non-finite values. No bound on the sum of `observed` on one device may be relied on, other than what follows from the above.
Results may differ from the reference program's by a relative error of at most 0.0003.
Values sent between devices are 32-bit elements; how exact they have to be, the bound alone decides.
No kernel may reach another device: no remote copies, remote signals or barrier semaphores. Data moves between devices by JAX's collectives and lax.ppermute only.
A program may use at most 128 MiB of HBM per device.

```python
import math
import jax
import jax.numpy as jnp
from jax import lax

LATENTS = 4
OUTS = 512
PAIRS = 256
STATE = 512
STEPS = 48


def draw_blend_matrix(key, part):
    noise = jax.random.normal(jax.random.fold_in(key, 11), (STATE, STATE), jnp.float32)
    symmetric = (noise + noise.T) * 0.70710678
    identity = jnp.eye(STATE, dtype=jnp.float32)
    return 0.08 * (identity + 0.3 / STATE ** 0.5 * symmetric)


def set_ends(array, rng, least, high):
    shape = array.shape
    place = [jax.random.randint(jax.random.fold_in(rng, axis), (), 0, shape[axis]) for axis in range(len(shape))]
    array = array.at[tuple(place)].set(least)
    longest = shape.index(max(shape))
    place[longest] = (place[longest] + 1) % shape[longest]
    return array.at[tuple(place)].set(high)


def block_scale(rng, dims, pieces, low, top_value):
    gain = 1.0
    for dim, shards_of in pieces:
        steps = jax.random.uniform(jax.random.fold_in(jax.random.fold_in(rng, 6), dim), (shards_of,), jnp.float32, low / len(pieces), top_value / len(pieces))
        gain = gain * jnp.repeat(jnp.exp(steps), dims[dim] // shards_of).reshape((-1,) + (1,) * (len(dims) - 1 - dim))
    return gain


def scatter_about(rng, shape, width, most, shards=(), held_as=jnp.bfloat16):
    array = jax.random.normal(rng, shape, jnp.float32) * width
    if len(shards) > 0:
        array = block_scale(rng, shape, shards, -0.22, 0.18) * array
    return jnp.clip(array, min=-most, max=most).astype(held_as)


def setup_inputs(seed: int = 0) -> dict:
    key_list = jax.random.split(jax.random.key(seed), 9)
    observations = scatter_about(key_list[0], (STEPS, OUTS), 1.0, 6.0, ((0, 4), (1, 2)), jnp.float32)
    observed = set_ends((jax.random.randint(key_list[1], (STEPS, OUTS), 0, 4) < 3).astype(jnp.int32), jax.random.fold_in(key_list[1], 1), 0, 1)
    loadings = scatter_about(key_list[2], (STEPS, OUTS, STATE), STATE ** -0.5, 0.25, ((0, 4), (1, 2)), jnp.float32)
    noise_precision = jnp.clip(jnp.exp(math.log(1.0) - 1.3862944 * jax.random.uniform(key_list[3], (OUTS,), jnp.float32) ** block_scale(key_list[3], (OUTS,), ((0, 2),), -0.2, 0.2)), 0.25, 1.0)
    blend_matrix = draw_blend_matrix(jax.random.fold_in(key_list[8], 71), 0)
    latent_rates = jnp.clip(jnp.exp(jax.random.uniform(key_list[5], (LATENTS,), jnp.float32, math.log(0.03), math.log(1.0))), 0.03, 1.0)
    pair_latent = set_ends(jax.random.randint(key_list[6], (PAIRS,), 0, LATENTS), jax.random.fold_in(key_list[6], 1), 0, LATENTS - 1).astype(jnp.int32)
    initial_mean = scatter_about(key_list[7], (STATE,), 1.0, 6.0, (), jnp.float32)
    return dict(observations=observations, observed=observed, loadings=loadings, noise_precision=noise_precision, blend_matrix=blend_matrix, latent_rates=latent_rates, pair_latent=pair_latent, initial_mean=initial_mean)


HIGHEST_PRECISION = lax.Precision.HIGHEST


def transition_parts(latent_rates, pair_latent):
    latent_ids = jnp.arange(latent_rates.shape[0], dtype=jnp.int32)
    one_hot = (pair_latent[:, None] == latent_ids[None, :]).astype(jnp.float32)
    pair_rate = jnp.sum(one_hot * latent_rates[None, :], axis=1)
    damping = jnp.exp(-pair_rate)
    diagonal_part = jnp.stack([damping * (1.0 + pair_rate), damping * (1.0 - pair_rate)], axis=1).reshape(-1)
    cross_part = jnp.stack([damping, -damping * pair_rate * pair_rate], axis=1).reshape(-1)
    return diagonal_part, cross_part


def right_transition(matrix, diagonal_part, cross_part):
    full_shape = matrix.shape
    swapped = matrix.reshape(full_shape[:-1] + (full_shape[-1] // 2, 2))[..., ::-1].reshape(full_shape)
    return matrix * diagonal_part + swapped * cross_part


def reference(observations, observed, loadings, noise_precision, blend_matrix, latent_rates, pair_latent, initial_mean):
    diagonal_part, cross_part = transition_parts(latent_rates, pair_latent)
    weight = observed.astype(jnp.float32) * noise_precision[None, :]
    identity = jnp.eye(loadings.shape[2], dtype=jnp.float32)

    def advance(state_in, inputs):
        row_weight, readings, step_loadings = inputs
        scaled = step_loadings * row_weight[:, None]
        info_matrix = jnp.dot(step_loadings.T, scaled, precision=HIGHEST_PRECISION)
        info_vector = jnp.dot(row_weight * readings, step_loadings, precision=HIGHEST_PRECISION)
        transit = right_transition(identity - jnp.dot(info_matrix, blend_matrix, precision=HIGHEST_PRECISION), diagonal_part, cross_part)
        shift = right_transition(jnp.dot(info_vector, blend_matrix, precision=HIGHEST_PRECISION), diagonal_part, cross_part)
        state_new = jnp.dot(state_in, transit, precision=HIGHEST_PRECISION) + shift
        reading = jnp.dot(step_loadings, state_new, precision=HIGHEST_PRECISION)
        return state_new, (state_new, reading)

    _, outputs = lax.scan(advance, initial_mean, (weight, observations, loadings))
    states, predicted = outputs
    return states, predicted
```

```python
import functools

import jax
import jax.numpy as jnp
from jax import lax
from jax.experimental import pallas as pl
from jax.experimental.pallas import tpu as pltpu
from jax.sharding import PartitionSpec as P

F32, BF16 = jnp.float32, jnp.bfloat16
VMEM_LIMIT = 12 * 2**20
CHUNK = 3
WHOLE = pl.BlockSpec(memory_space=pltpu.VMEM)
SCALARS = pl.BlockSpec(memory_space=pltpu.SMEM)
FAR = pl.BlockSpec(memory_space=pltpu.HBM)


def call(kernel, name, outs, in_specs, scratch=(), flops=0, moved=0):
    return pl.pallas_call(
        kernel,
        out_shape=outs,
        in_specs=in_specs,
        out_specs=[WHOLE] * len(outs),
        scratch_shapes=scratch,
        compiler_params=pltpu.CompilerParams(vmem_limit_bytes=VMEM_LIMIT),
        cost_estimate=pl.CostEstimate(flops=flops, bytes_accessed=moved, transcendentals=0),
        name=name,
    )


def kept(*shape, dtype=F32):
    return pltpu.VMEM(shape, dtype)


def swap_pairs(x):
    width = x.shape[-1]
    lane = lax.broadcasted_iota(jnp.int32, x.shape, 1)
    return jnp.where(lane % 2 == 0, pltpu.roll(x, width - 1, 1), pltpu.roll(x, 1, 1))


def halves(x):
    high = x.astype(BF16)
    return high, (x - high.astype(F32)).astype(BF16)


def times_gain(scaled, gain_high, gain_low):
    high, low = halves(scaled)
    dot = functools.partial(jnp.dot, preferred_element_type=F32)
    return dot(high, gain_high) + (dot(high, gain_low) + dot(low, gain_high))


def gain_step(load, weight, reading, gain_high, gain_low):
    gained = times_gain(load * weight, gain_high, gain_low)
    return gained, jnp.sum(reading * gained, axis=0, keepdims=True)


def own_kernel(
    steps, rates, pairs, blend, columns, loads_far,
    loads, gained, shift, parts, gain_high, gain_low, sems,
):
    copies = [
        pltpu.make_async_copy(loads_far.at[k], loads.at[k], sems.at[k]) for k in range(steps)
    ]
    for copy in copies:
        copy.start()
    width = blend.shape[1]
    layout = pairs[...]
    rate = jnp.zeros(layout.shape, F32)
    for latent in range(rates.shape[0]):
        rate = jnp.where(layout == latent, rates[latent], rate)
    spread = lax.broadcasted_iota(jnp.int32, (layout.shape[1], width), 1) // 2
    spread = spread == lax.broadcasted_iota(jnp.int32, spread.shape, 0)
    rate = jnp.dot(
        jnp.broadcast_to(rate, (8, layout.shape[1])),
        spread.astype(F32),
        precision=lax.Precision.HIGHEST,
        preferred_element_type=F32,
    )
    even = lax.broadcasted_iota(jnp.int32, rate.shape, 1) % 2 == 0
    damping = jnp.exp(-rate)
    diagonal = jnp.where(even, damping * (1.0 + rate), damping * (1.0 - rate))
    cross = jnp.where(even, damping, -damping * rate * rate)
    parts[0] = diagonal
    parts[1] = cross
    gain = blend[...]
    gain = gain * diagonal[0:1] + swap_pairs(gain) * cross[0:1]
    high, low = halves(gain)
    gain_high[...] = high
    gain_low[...] = low
    for k in range(steps):
        copies[k].wait()
        gained[k], shift[k : k + 1, :] = gain_step(
            loads[k], columns[:, k : k + 1], columns[:, steps + k : steps + k + 1], high, low
        )


def advance(state, loads, gained, shift, diagonal, cross):
    width = state.shape[1]
    drift = shift
    for load, gain in zip(loads, gained):
        total = jnp.zeros_like(state)
        for row in range(0, load.shape[0], 8):
            product = load[row : row + 8, :] * state
            reading = jnp.sum(product, axis=1, keepdims=True)
            total = total + reading * gain[row : row + 8, :]
        drift = drift - jnp.sum(total, axis=0, keepdims=True)
    return state * diagonal + swap_pairs(state) * cross + drift


def part_kernel(
    first, count, steps, entering, loads_far, columns, loads_own, gained_own, shift_own, parts,
    gain_high, gain_low, loads, gained, shift, states, leaving, sems,
):
    copies = [
        pltpu.make_async_copy(loads_far.at[k], loads.at[k], sems.at[k]) for k in range(count)
    ]
    for copy in copies:
        copy.start()
    state = jnp.broadcast_to(entering[0:1, :], parts.shape[1:])
    high, low = gain_high[...], gain_low[...]
    for k in range(count):
        at = first + k
        copies[k].wait()
        gained[k], other = gain_step(
            loads[k], columns[:, at : at + 1], columns[:, steps + at : steps + at + 1], high, low
        )
        own = shift_own[at : at + 1, :]
        shift[k : k + 1, :] = own + other
        state = advance(
            state,
            (loads_own.at[at], loads.at[k]),
            (gained_own.at[at], gained.at[k]),
            own + other,
            parts[0],
            parts[1],
        )
        states[k : k + 1, :] = state[0:1, :]
    leaving[...] = state


def chain(entering, loads_own, gained_own, loads, gained, shifts, parts, states):
    state = jnp.broadcast_to(entering[0:1, :], parts.shape[1:])
    at = 0
    for load, gain, shift in zip(loads, gained, shifts):
        for k in range(load.shape[0]):
            state = advance(
                state,
                (loads_own.at[at], load.at[k]),
                (gained_own.at[at], gain.at[k]),
                shift[k : k + 1, :],
                parts[0],
                parts[1],
            )
            states[at : at + 1, :] = state[0:1, :]
            at += 1
    return state


def block_kernel(turn, count, position, before, entering, parts, loads_own, gained_own, *rest):
    loads, gained, shifts = rest[:count], rest[count : 2 * count], rest[2 * count : 3 * count]
    states, leaving = rest[3 * count :]

    @pl.when(position[0] == turn)
    def _():
        leaving[...] = chain(
            entering, loads_own, gained_own, loads, gained, shifts, parts, states
        )

    @pl.when(position[0] != turn)
    def _():
        states[...] = before[...]
        leaving[...] = jnp.zeros_like(leaving)


def last_kernel(turn, count, position, before, entering, parts, loads_own, gained_own, *rest):
    loads, gained, shifts = rest[:count], rest[count : 2 * count], rest[2 * count : 3 * count]
    own_states, predicted, states, columns = rest[3 * count :]

    @pl.when(position[0] == turn)
    def _():
        chain(entering, loads_own, gained_own, loads, gained, shifts, parts, states)

    @pl.when(position[0] != turn)
    def _():
        states[...] = before[...]

    share = own_states.shape[1]
    start = pl.multiple_of(position[1] * share, share)
    own_states[...] = states[:, pl.ds(start, share)]
    steps = states.shape[0]
    for k in range(steps):
        columns[:, k : k + 1] = jnp.sum(
            loads_own[k] * states[k : k + 1, :], axis=1, keepdims=True
        )
    predicted[...] = columns[...].T[:steps, :]


def per_device(
    observations, observed, loadings, noise_precision, blend_matrix, latent_rates, pair_latent,
    initial_mean,
):
    steps, outs, width = loadings.shape
    blocks = lax.axis_size("tm")
    share = width // lax.axis_size("state")
    other = functools.partial(lax.ppermute, axis_name="outputs", perm=[(0, 1), (1, 0)])
    weight = observed.astype(F32) * noise_precision[None, :]
    columns = jnp.concatenate([weight, observations], axis=0).T
    columns_far = other(columns)
    starts = range(0, steps, CHUNK)
    loads_far = [other(loadings[at : at + CHUNK]) for at in starts]
    initial = jnp.broadcast_to(initial_mean[None, :], (8, width))
    position = jnp.stack([lax.axis_index("tm"), lax.axis_index("state")]).astype(jnp.int32)

    half = 2 * 3 * outs * width * width
    loads_own, gained_own, shift_own, parts, gain_high, gain_low = call(
        functools.partial(own_kernel, steps),
        "own_half",
        [
            kept(steps, outs, width),
            kept(steps, outs, width),
            kept(steps, width),
            kept(2, 8, width),
            kept(width, width, dtype=BF16),
            kept(width, width, dtype=BF16),
        ],
        [SCALARS, WHOLE, WHOLE, WHOLE, FAR],
        [pltpu.SemaphoreType.DMA((steps,))],
        flops=steps * half,
        moved=4 * steps * outs * width,
    )(latent_rates, pair_latent[None, :], blend_matrix, columns, loadings)

    leaving = initial
    loads, gained, shifts, states = [], [], [], []
    for at, far in zip(starts, loads_far):
        count = far.shape[0]
        load, gain, shift, state, leaving = call(
            functools.partial(part_kernel, at, count, steps),
            "other_half",
            [
                kept(count, outs, width),
                kept(count, outs, width),
                kept(count, width),
                jax.ShapeDtypeStruct((count, width), F32),
                jax.ShapeDtypeStruct((8, width), F32),
            ],
            [WHOLE, FAR] + [WHOLE] * 7,
            [pltpu.SemaphoreType.DMA((count,))],
            flops=count * half,
            moved=4 * count * outs * width,
        )(
            leaving, far, columns_far, loads_own, gained_own, shift_own, parts, gain_high,
            gain_low,
        )
        loads.append(load)
        gained.append(gain)
        shifts.append(shift)
        states.append(state)
    states = jnp.concatenate(states, axis=0)
    parted = (*loads, *gained, *shifts)
    specs = [SCALARS] + [WHOLE] * (5 + len(parted))
    work = dict(flops=steps * half, moved=0)
    for turn in range(1, blocks):
        entering = lax.ppermute(leaving, "tm", [(turn - 1, turn)])
        operands = (position, states, entering, parts, loads_own, gained_own, *parted)
        if turn < blocks - 1:
            states, leaving = call(
                functools.partial(block_kernel, turn, len(loads)),
                "block_chain",
                [
                    jax.ShapeDtypeStruct((steps, width), F32),
                    jax.ShapeDtypeStruct((8, width), F32),
                ],
                specs,
                **work,
            )(*operands)
    if blocks == 1:
        operands = (position, states, initial, parts, loads_own, gained_own, *parted)
    return tuple(
        call(
            functools.partial(last_kernel, blocks - 1 if blocks > 1 else -1, len(loads)),
            "last_chain",
            [
                jax.ShapeDtypeStruct((steps, share), F32),
                jax.ShapeDtypeStruct((steps, outs), F32),
            ],
            specs,
            [pltpu.VMEM((steps, width), F32), pltpu.VMEM((outs, 128), F32)],
            **work,
        )(*operands)
    )


def solution(mesh):
    placed = (
        P("tm", "outputs"),
        P("tm", "outputs"),
        P("tm", "outputs", None),
        P("outputs"),
        P(),
        P(),
        P(),
        P(),
    )
    return jax.shard_map(
        per_device,
        mesh=mesh,
        in_specs=placed,
        out_specs=(P("tm", "state"), P("tm", "outputs")),
        check_vma=False,
    )
```

```python
import functools

import jax
import jax.numpy as jnp
from jax import lax
from jax.experimental import pallas as pl
from jax.experimental.pallas import tpu as pltpu
from jax.sharding import PartitionSpec as P

F32, BF16 = jnp.float32, jnp.bfloat16
VMEM_LIMIT = 8 * 2**20
LAST_PART = 1
PARTS = 4
SECOND_GAINS = 5
WHOLE = pl.BlockSpec(memory_space=pltpu.VMEM)
FAR = pl.BlockSpec(memory_space=pl.ANY)


def call(kernel, name, outs, in_specs, scratch=(), flops=0, moved=0):
    return pl.pallas_call(
        kernel,
        out_shape=outs,
        in_specs=in_specs,
        out_specs=[WHOLE] * len(outs),
        scratch_shapes=scratch,
        compiler_params=pltpu.CompilerParams(vmem_limit_bytes=VMEM_LIMIT),
        cost_estimate=pl.CostEstimate(flops=flops, bytes_accessed=moved, transcendentals=0),
        name=name,
    )


def kept(*shape, dtype=F32):
    return pltpu.VMEM(shape, dtype)


def swap_pairs(x):
    width = x.shape[-1]
    lane = lax.broadcasted_iota(jnp.int32, x.shape, 1)
    return jnp.where(lane % 2 == 0, pltpu.roll(x, width - 1, 1), pltpu.roll(x, 1, 1))


def halves(x):
    high = x.astype(BF16)
    return high, (x - high.astype(F32)).astype(BF16)


def times_gain(scaled, gain_high, gain_low):
    high, low = halves(scaled)
    dot = functools.partial(jnp.dot, preferred_element_type=F32)
    return dot(high, gain_high) + (dot(high, gain_low) + dot(low, gain_high))


def part_sizes(steps):
    rest = steps - LAST_PART
    sizes = [rest // (PARTS - 1) + (i < rest % (PARTS - 1)) for i in range(PARTS - 1)]
    return sizes + [LAST_PART]


def copied(source, target, sem):
    copy = pltpu.make_async_copy(source, target, sem)
    copy.start()
    return copy


def fetched(loads_far, first, loads, sems):
    return [
        copied(loads_far.at[first + k], loads.at[k], sems.at[k]) for k in range(loads.shape[0])
    ]


def scale(copies, first, steps, loads, columns, scaled, sent):
    outs = loads.shape[1]
    for k, copy in enumerate(copies):
        at = first + k
        copy.wait()
        rows = loads[k] * columns[:, at : at + 1]
        tail = jnp.sum(columns[:, steps + at : steps + at + 1] * rows, axis=0, keepdims=True)
        tail = jnp.broadcast_to(tail, (8, tail.shape[1]))
        for target in (sent, scaled):
            target[k, :outs, :] = rows
            target[k, outs:, :] = tail


def stage_kernel(
    loads_far, observed_far, observations_far, noise_far, loads, scaled, sent, columns,
    observed, observations, noise, turned, sems, small_sems,
):
    small = [
        copied(source, target, small_sems.at[i])
        for i, (source, target) in enumerate(
            (
                (observed_far, observed),
                (observations_far, observations),
                (noise_far, noise),
            )
        )
    ]
    copies = fetched(loads_far, 0, loads, sems)
    turned[...] = jnp.zeros_like(turned)
    for copy in small:
        copy.wait()
    steps = observed.shape[0]
    root = jnp.sqrt(observed[...].astype(F32) * noise[...])
    turned[:steps, :] = root
    turned[steps : 2 * steps, :] = root * observations[...]
    columns[...] = turned[...].T
    scale(copies, 0, steps, loads, columns, scaled, sent)


def transition(rates, pairs, width):
    layout = pairs[...]
    rate = jnp.zeros(layout.shape, F32)
    for latent in range(rates.shape[1]):
        rate = jnp.where(layout == latent, rates[:, latent : latent + 1], rate)
    spread = lax.broadcasted_iota(jnp.int32, (layout.shape[1], width), 1) // 2
    spread = spread == lax.broadcasted_iota(jnp.int32, spread.shape, 0)
    rate = jnp.dot(
        jnp.broadcast_to(rate, (8, layout.shape[1])),
        spread.astype(F32),
        precision=lax.Precision.HIGHEST,
        preferred_element_type=F32,
    )
    even = lax.broadcasted_iota(jnp.int32, rate.shape, 1) % 2 == 0
    damping = jnp.exp(-rate)
    diagonal = jnp.where(even, damping * (1.0 + rate), damping * (1.0 - rate))
    cross = jnp.where(even, damping, -damping * rate * rate)
    return diagonal, cross


def gain_limit(block, steps):
    return (0, min(SECOND_GAINS, steps), steps)[min(block, 2)]


def by_block(work, steps):
    block = lax.axis_index("tm")
    for i in (1, 2):

        @pl.when(block == 1 if i == 1 else block > 1)
        def _():
            work(gain_limit(i, steps))


def fill_gains(limit, first, scaled, gain_high, gain_low, gained):
    rows = scaled.shape[1]
    for k in range(min(scaled.shape[0], limit - first)):
        block = jnp.concatenate([scaled[k], scaled[k, rows - 8 :, :]], axis=0)
        gained[k] = times_gain(block, gain_high[...], gain_low[...])[:rows]


def second_kernel(
    first, steps, loads_far, columns, rates, pairs, blend,
    loads, scaled, sent, parts, gain_high, gain_low, sems,
):
    copies = fetched(loads_far, first, loads, sems)
    diagonal, cross = transition(rates, pairs, blend.shape[1])
    parts[0] = diagonal
    parts[1] = cross

    @pl.when(lax.axis_index("tm") != 0)
    def _():
        gain = blend[...]
        gain = gain * diagonal[0:1] + swap_pairs(gain) * cross[0:1]
        gain_high[...], gain_low[...] = halves(gain)

    scale(copies, first, steps, loads, columns, scaled, sent)


def third_kernel(
    firsts, steps, loads_far, columns, scaled_first, gain_high, gain_low,
    gained_first, *rest,
):
    count = len(firsts)
    groups = [rest[3 * i : 3 * i + 3] for i in range(count)]
    sems = rest[3 * count :]
    copies = [
        fetched(loads_far, first, group[0], sem)
        for first, group, sem in zip(firsts, groups, sems)
    ]

    def work(limit):
        fill_gains(limit, 0, scaled_first, gain_high, gain_low, gained_first)

    by_block(work, steps)
    for first, group, copy in zip(firsts, groups, copies):
        loads, scaled, sent = group
        scale(copy, first, steps, loads, columns, scaled, sent)


def gain_kernel(firsts, steps, gain_high, gain_low, *rest):
    count = len(firsts)

    def work(limit):
        for first, scaled, gained in zip(firsts, rest[:count], rest[count:]):
            fill_gains(limit, first, scaled, gain_high, gain_low, gained)

    by_block(work, steps)


def reflected(state, pull, blend):
    pull = jnp.broadcast_to(pull, state.shape)
    place = lax.broadcasted_iota(jnp.int32, (8, 128), 1) - lax.broadcasted_iota(
        jnp.int32, (8, 128), 0
    )
    turned = []
    for start in range(0, state.shape[1], 128):
        total = jnp.zeros((8, 128), F32)
        for row in range(0, 128, 8):
            blended = blend[start + row : start + row + 8, :] * pull
            total = total + jnp.where(
                place == row, jnp.sum(blended, axis=1, keepdims=True), 0.0
            )
        turned.append(jnp.sum(total, axis=0, keepdims=True))
    return state - jnp.concatenate(turned, axis=1)


def advance(state, scaled, gained, parts, blend=None):
    pull = 0.0
    for rows, gains in zip(scaled, gained):
        outs = rows.shape[0] - 8
        total = jnp.zeros_like(state)
        for row in range(0, outs, 8):
            block = rows[row : row + 8, :]
            reading = jnp.sum(block * state, axis=1, keepdims=True)
            total = total + reading * (block if blend is not None else gains[row : row + 8, :])
        pull += jnp.sum(total, axis=0, keepdims=True) - gains[outs : outs + 1, :]
    if blend is not None:
        state, pull = reflected(state, pull, blend), 0.0
    return state * parts[0] + swap_pairs(state) * parts[1] - pull


def part_kernel(
    first, steps, entering, scaled_far, scaled_own, parts, blend, gain_high, gain_low,
    scaled, gained, states, leaving, sem,
):
    copied(scaled_far, scaled, sem).wait()
    block = lax.axis_index("tm")

    @pl.when(block == 0)
    def _():
        state = jnp.broadcast_to(entering[0:1, :], parts.shape[1:])
        for k in range(scaled.shape[0]):
            pair = (scaled_own.at[k], scaled.at[k])
            state = advance(state, pair, pair, parts, blend)
            states[k : k + 1, :] = state[0:1, :]
        leaving[...] = state

    def work(limit):
        fill_gains(limit, first, scaled, gain_high, gain_low, gained)

    by_block(work, steps)


def chain(limit, entering, parts, blend, operands, states):
    state = jnp.broadcast_to(entering[0:1, :], parts.shape[1:])
    at = 0
    for _, own, gained_own, scaled, gained in operands:
        for k in range(own.shape[0]):
            pair = (own.at[k], scaled.at[k])
            if at < limit:
                state = advance(state, pair, (gained_own.at[k], gained.at[k]), parts)
            else:
                state = advance(state, pair, pair, parts, blend)
            states[at : at + 1, :] = state[0:1, :]
            at += 1
    return state


def grouped(refs, count):
    return [refs[5 * i : 5 * i + 5] for i in range(count)], refs[5 * count :]


def block_kernel(turn, count, before, entering, parts, blend, *refs):
    operands, (states, leaving) = grouped(refs, count)
    block = lax.axis_index("tm")

    @pl.when(block == turn)
    def _():
        limit = gain_limit(turn, states.shape[0])
        leaving[...] = chain(limit, entering, parts, blend, operands, states)

    @pl.when(block != turn)
    def _():
        states[...] = before[...]
        leaving[...] = jnp.zeros_like(leaving)


def last_kernel(turn, count, before, entering, parts, blend, *refs):
    operands, (own_states, predicted, states, readings) = grouped(refs, count)
    block = lax.axis_index("tm")

    @pl.when(block == turn)
    def _():
        limit = gain_limit(turn, states.shape[0])
        chain(limit, entering, parts, blend, operands, states)

    @pl.when(block != turn)
    def _():
        states[...] = before[...]

    share = own_states.shape[1]
    start = pl.multiple_of(lax.axis_index("state") * share, share)
    own_states[...] = states[:, pl.ds(start, share)]
    at = 0
    for loads, *_ in operands:
        for k in range(loads.shape[0]):
            readings[:, at : at + 1] = jnp.sum(
                loads[k] * states[at : at + 1, :], axis=1, keepdims=True
            )
            at += 1
    predicted[...] = readings[...].T[:at, :]


def per_device(
    observations, observed, loadings, noise_precision, blend_matrix, latent_rates, pair_latent,
    initial_mean,
):
    steps, outs, width = loadings.shape
    blocks = lax.axis_size("tm")
    share = width // lax.axis_size("state")
    other = functools.partial(lax.ppermute, axis_name="outputs", perm=[(0, 1), (1, 0)])
    in_hbm = functools.partial(
        pltpu.with_memory_space_constraint, memory_space=pltpu.HBM
    )
    loadings = in_hbm(loadings)
    sizes = part_sizes(steps)
    count = len(sizes)
    firsts = [sum(sizes[:i]) for i in range(count)]
    initial = jnp.broadcast_to(initial_mean[None, :], (8, width))

    half = 2 * 3 * outs * width * width
    vector, gain_type = kept(8, width), kept(width, width, dtype=BF16)
    sems = pltpu.SemaphoreType.DMA

    def matrices(size):
        return kept(size, outs + 8, width)

    def chunk(size):
        return [kept(size, outs, width), matrices(size), matrices(size)]

    small = (steps, outs)
    *first_chunk, columns = call(
        stage_kernel,
        "stage",
        chunk(sizes[0]) + [kept(outs, 128)],
        [FAR] * 4,
        [
            pltpu.VMEM(small, observed.dtype),
            pltpu.VMEM(small, F32),
            pltpu.VMEM((1, outs), F32),
            pltpu.VMEM((128, outs), F32),
            sems((sizes[0],)),
            sems((3,)),
        ],
        moved=8 * sizes[0] * outs * width,
    )(loadings, in_hbm(observed), in_hbm(observations), in_hbm(noise_precision[None, :]))
    *second_chunk, parts, gain_high, gain_low = call(
        functools.partial(second_kernel, firsts[1], steps),
        "second_part",
        chunk(sizes[1]) + [kept(2, 8, width), gain_type, gain_type],
        [FAR] + [WHOLE] * 4,
        [sems((sizes[1],))],
        moved=8 * sizes[1] * outs * width,
    )(loadings, columns, latent_rates[None, :], pair_latent[None, :], blend_matrix)
    gained_first, *later = call(
        functools.partial(third_kernel, firsts[2:], steps),
        "later_parts",
        [matrices(sizes[0])] + sum([chunk(size) for size in sizes[2:]], []),
        [FAR] + [WHOLE] * 4,
        [sems((size,)) for size in sizes[2:]],
        flops=sizes[0] * half,
        moved=8 * sum(sizes[2:]) * outs * width,
    )(loadings, columns, first_chunk[1], gain_high, gain_low)
    chunks = [first_chunk, second_chunk] + [later[i : i + 3] for i in range(0, len(later), 3)]
    loads_own, scaled_own, sent = zip(*chunks)
    gained_own = [gained_first] + list(
        call(
            functools.partial(gain_kernel, firsts[1:], steps),
            "own_gains",
            [matrices(size) for size in sizes[1:]],
            [WHOLE] * (1 + count),
            flops=sum(sizes[1:]) * half,
        )(gain_high, gain_low, *scaled_own[1:])
    )

    leaving = initial
    operands, states = [], []
    for i in range(count):
        scaled, gained, state, leaving = call(
            functools.partial(part_kernel, firsts[i], steps),
            "other_part",
            [matrices(sizes[i]), matrices(sizes[i]), kept(sizes[i], width), vector],
            [WHOLE, FAR] + [WHOLE] * 5,
            [sems],
            flops=sizes[i] * half,
            moved=8 * sizes[i] * outs * width,
        )(
            leaving, other(sent[i]), scaled_own[i], parts, blend_matrix, gain_high, gain_low
        )
        operands += [loads_own[i], scaled_own[i], gained_own[i], scaled, gained]
        states.append(state)
    states = jnp.concatenate(states, axis=0)

    specs = [WHOLE] * (4 + len(operands))
    entering = leaving
    for turn in range(1, blocks):
        entering = lax.ppermute(leaving, "tm", [(turn - 1, turn)])
        if turn < blocks - 1:
            states, leaving = call(
                functools.partial(block_kernel, turn, count),
                "block_chain",
                [kept(steps, width), vector],
                specs,
                flops=steps * half,
            )(states, entering, parts, blend_matrix, *operands)
    return tuple(
        call(
            functools.partial(last_kernel, blocks - 1 if blocks > 1 else -1, count),
            "last_chain",
            [
                jax.ShapeDtypeStruct((steps, share), F32),
                jax.ShapeDtypeStruct((steps, outs), F32),
            ],
            specs,
            [pltpu.VMEM((steps, width), F32), pltpu.VMEM((outs, 128), F32)],
            flops=steps * half,
        )(states, entering, parts, blend_matrix, *operands)
    )


def solution(mesh):
    placed = (
        P("tm", "outputs"),
        P("tm", "outputs"),
        P("tm", "outputs", None),
        P("outputs"),
        P(),
        P(),
        P(),
        P(),
    )
    return jax.shard_map(
        per_device,
        mesh=mesh,
        in_specs=placed,
        out_specs=(P("tm", "state"), P("tm", "outputs")),
        check_vma=False,
    )
```

```python
import functools

import jax
import jax.numpy as jnp
from jax import lax
from jax.experimental import pallas as pl
from jax.experimental.pallas import tpu as pltpu
from jax.sharding import PartitionSpec as P

F32, BF16 = jnp.float32, jnp.bfloat16
VMEM_LIMIT = 8 * 2**20
LAST_PART = 1
PARTS = 4
GAIN_STEPS = (0, 8, 10)
EARLY_STEPS = (0, 4, 2)
WHOLE = pl.BlockSpec(memory_space=pltpu.VMEM)
FAR = pl.BlockSpec(memory_space=pl.ANY)


def call(kernel, name, outs, in_specs, scratch=(), flops=0, moved=0):
    return pl.pallas_call(
        kernel,
        out_shape=outs,
        in_specs=in_specs,
        out_specs=[WHOLE] * len(outs),
        scratch_shapes=scratch,
        compiler_params=pltpu.CompilerParams(vmem_limit_bytes=VMEM_LIMIT),
        cost_estimate=pl.CostEstimate(flops=flops, bytes_accessed=moved, transcendentals=0),
        name=name,
    )


def kept(*shape, dtype=F32):
    return pltpu.VMEM(shape, dtype)


def swap_pairs(x):
    width = x.shape[-1]
    lane = lax.broadcasted_iota(jnp.int32, x.shape, 1)
    return jnp.where(lane % 2 == 0, pltpu.roll(x, width - 1, 1), pltpu.roll(x, 1, 1))


def halves(x):
    high = x.astype(BF16)
    return high, (x - high.astype(F32)).astype(BF16)


def times_gain(scaled, gain_high, gain_low):
    high, low = halves(scaled)
    dot = functools.partial(jnp.dot, preferred_element_type=F32)
    return dot(high, gain_high) + (dot(high, gain_low) + dot(low, gain_high))


def part_sizes(steps):
    rest = steps - LAST_PART
    sizes = [(rest + PARTS - 2 - i) // (PARTS - 1) for i in range(PARTS - 1)]
    return sizes + [LAST_PART]


def copied(source, target, sem):
    copy = pltpu.make_async_copy(source, target, sem)
    copy.start()
    return copy


def fetched(loads_far, first, loads, sems):
    return [
        copied(loads_far.at[first + k], loads.at[k], sems.at[k]) for k in range(loads.shape[0])
    ]


def scale(copies, first, steps, loads, columns, scaled, sent):
    outs = loads.shape[1]
    for k, copy in enumerate(copies):
        at = first + k
        copy.wait()
        rows = loads[k] * columns[:, at : at + 1]
        tail = jnp.sum(columns[:, steps + at : steps + at + 1] * rows, axis=0, keepdims=True)
        tail = jnp.broadcast_to(tail, (8, tail.shape[1]))
        for target in (sent, scaled):
            target[k, :outs, :] = rows
            target[k, outs:, :] = tail


def stage_kernel(
    loads_far, observed_far, observations_far, noise_far, loads, scaled, sent, columns,
    observed, observations, noise, turned, sems, small_sems,
):
    small = [
        copied(source, target, small_sems.at[i])
        for i, (source, target) in enumerate(
            (
                (observed_far, observed),
                (observations_far, observations),
                (noise_far, noise),
            )
        )
    ]
    copies = fetched(loads_far, 0, loads, sems)
    turned[...] = jnp.zeros_like(turned)
    for copy in small:
        copy.wait()
    steps = observed.shape[0]
    root = jnp.sqrt(observed[...].astype(F32) * noise[...])
    turned[:steps, :] = root
    turned[steps : 2 * steps, :] = root * observations[...]
    columns[...] = turned[...].T
    scale(copies, 0, steps, loads, columns, scaled, sent)


def transition(rates, pairs, width):
    layout = pairs[...]
    rate = jnp.zeros(layout.shape, F32)
    for latent in range(rates.shape[1]):
        rate = jnp.where(layout == latent, rates[:, latent : latent + 1], rate)
    spread = lax.broadcasted_iota(jnp.int32, (layout.shape[1], width), 1) // 2
    spread = spread == lax.broadcasted_iota(jnp.int32, spread.shape, 0)
    rate = jnp.dot(
        jnp.broadcast_to(rate, (8, layout.shape[1])),
        spread.astype(F32),
        precision=lax.Precision.HIGHEST,
        preferred_element_type=F32,
    )
    even = lax.broadcasted_iota(jnp.int32, rate.shape, 1) % 2 == 0
    damping = jnp.exp(-rate)
    diagonal = jnp.where(even, damping * (1.0 + rate), damping * (1.0 - rate))
    cross = jnp.where(even, damping, -damping * rate * rate)
    return diagonal, cross


def gain_limit(block, steps):
    return min(GAIN_STEPS[block], steps) if block < len(GAIN_STEPS) else steps


def early_limit(block, size):
    return min(EARLY_STEPS[min(block, len(EARLY_STEPS) - 1)], size)


def by_block(work, steps):
    block = lax.axis_index("tm")
    kinds = min(len(GAIN_STEPS), lax.axis_size("tm") - 1)
    for i in range(1, kinds + 1):

        @pl.when(block == i if i < kinds else block >= i)
        def _():
            work(i, gain_limit(i, steps))


def fill_gains(limit, first, scaled, gain_high, gain_low, gained, begin=0):
    rows = scaled.shape[1]
    for k in range(begin, min(scaled.shape[0], limit - first)):
        block = jnp.concatenate([scaled[k], scaled[k, rows - 8 :, :]], axis=0)
        gained[k] = times_gain(block, gain_high[...], gain_low[...])[:rows]


def second_kernel(
    first, steps, loads_far, columns, rates, pairs, blend, mean,
    loads, scaled, sent, parts, gain_high, gain_low, initial, sems,
):
    copies = fetched(loads_far, first, loads, sems)
    diagonal, cross = transition(rates, pairs, blend.shape[1])
    parts[0] = diagonal
    parts[1] = cross
    initial[...] = jnp.broadcast_to(mean[...], initial.shape)

    @pl.when(lax.axis_index("tm") != 0)
    def _():
        gain = blend[...]
        gain = gain * diagonal[0:1] + swap_pairs(gain) * cross[0:1]
        gain_high[...], gain_low[...] = halves(gain)

    scale(copies, first, steps, loads, columns, scaled, sent)


def third_kernel(
    firsts, steps, loads_far, columns, scaled_first, gain_high, gain_low,
    gained_first, *rest,
):
    count = len(firsts)
    groups = [rest[3 * i : 3 * i + 3] for i in range(count)]
    sems = rest[3 * count :]
    copies = [
        fetched(loads_far, first, group[0], sem)
        for first, group, sem in zip(firsts, groups, sems)
    ]

    def work(block, limit):
        fill_gains(limit, 0, scaled_first, gain_high, gain_low, gained_first)

    by_block(work, steps)
    for first, group, copy in zip(firsts, groups, copies):
        loads, scaled, sent = group
        scale(copy, first, steps, loads, columns, scaled, sent)


def gain_kernel(firsts, steps, gain_high, gain_low, *rest):
    count = len(firsts)

    def work(block, limit):
        for first, scaled, gained in zip(firsts, rest[:count], rest[count:]):
            fill_gains(limit, first, scaled, gain_high, gain_low, gained)

    by_block(work, steps)


def reflected(state, pull, blend):
    pull = jnp.broadcast_to(pull, state.shape)
    place = lax.broadcasted_iota(jnp.int32, (8, 128), 1) - lax.broadcasted_iota(
        jnp.int32, (8, 128), 0
    )
    turned = []
    for start in range(0, state.shape[1], 128):
        total = jnp.zeros((8, 128), F32)
        for row in range(0, 128, 8):
            blended = blend[start + row : start + row + 8, :] * pull
            total = total + jnp.where(
                place == row, jnp.sum(blended, axis=1, keepdims=True), 0.0
            )
        turned.append(jnp.sum(total, axis=0, keepdims=True))
    return state - jnp.concatenate(turned, axis=1)


def advance(state, scaled, gained, parts, blend=None):
    pull = 0.0
    for rows, gains in zip(scaled, gained):
        outs = rows.shape[0] - 8
        total = jnp.zeros_like(state)
        for row in range(0, outs, 8):
            block = rows[row : row + 8, :]
            reading = jnp.sum(block * state, axis=1, keepdims=True)
            total = total + reading * (block if blend is not None else gains[row : row + 8, :])
        pull += jnp.sum(total, axis=0, keepdims=True) - gains[outs : outs + 1, :]
    if blend is not None:
        state, pull = reflected(state, pull, blend), 0.0
    return state * parts[0] + swap_pairs(state) * parts[1] - pull


def part_kernel(
    early, steps, entering, scaled_far, scaled_own, parts, blend, gain_high, gain_low,
    scaled, states, leaving, *rest,
):
    *gained, sem = rest
    copied(scaled_far, scaled, sem).wait()
    block = lax.axis_index("tm")

    @pl.when(block == 0)
    def _():
        state = jnp.broadcast_to(entering[0:1, :], parts.shape[1:])
        for k in range(scaled.shape[0]):
            pair = (scaled_own.at[k], scaled.at[k])
            state = advance(state, pair, pair, parts, blend)
            states[k : k + 1, :] = state[0:1, :]
        leaving[...] = state

    def work(block, limit):
        fill_gains(
            early_limit(block, scaled.shape[0]), 0, scaled, gain_high, gain_low, *gained
        )

    if early:
        by_block(work, steps)


def late_kernel(firsts, steps, _, gain_high, gain_low, *rest):
    count = len(firsts)
    parts = list(zip(firsts, rest[:count], rest[count:]))

    def work(block, limit):
        for i, (first, scaled, gained) in enumerate(parts):
            begin = 0 if i else early_limit(block, scaled.shape[0])
            fill_gains(limit, first, scaled, gain_high, gain_low, gained, begin)

    by_block(work, steps)


def chain(turn, entering, parts, blend, operands, early, states, observe=None):
    limit = gain_limit(turn, states.shape[0])
    state = jnp.broadcast_to(entering[0:1, :], parts.shape[1:])
    at = 0
    for _, own, gained_own, scaled, gained in operands:
        for k in range(own.shape[0]):
            pair = (own.at[k], scaled.at[k])
            if at < limit:
                other = early if at < early_limit(turn, early.shape[0]) else gained
                state = advance(state, pair, (gained_own.at[k], other.at[k]), parts)
            else:
                state = advance(state, pair, pair, parts, blend)
            states[at : at + 1, :] = state[0:1, :]
            if observe is not None:
                observe(at, state)
            at += 1
    return state


def grouped(refs, count):
    return [refs[5 * i : 5 * i + 5] for i in range(count)], refs[5 * count :]


def block_kernel(turn, count, before, entering, parts, blend, early, *refs):
    operands, (states, leaving) = grouped(refs, count)
    block = lax.axis_index("tm")

    @pl.when(block == turn)
    def _():
        leaving[...] = chain(turn, entering, parts, blend, operands, early, states)

    @pl.when(block != turn)
    def _():
        states[...] = before[...]
        leaving[...] = jnp.zeros_like(leaving)


def last_kernel(turn, count, before, entering, parts, blend, early, *refs):
    operands, (own_states, predicted, states, readings) = grouped(refs, count)
    block = lax.axis_index("tm")
    rows = [loads.at[k] for loads, *_ in operands for k in range(loads.shape[0])]

    def observe(at, state):
        outs = rows[at].shape[0]
        for row in range(0, outs, 8):
            product = rows[at][row : row + 8, :] * state
            readings[row : row + 8, at : at + 1] = jnp.sum(product, axis=1, keepdims=True)

    @pl.when(block == turn)
    def _():
        chain(turn, entering, parts, blend, operands, early, states, observe)

    @pl.when(block != turn)
    def _():
        states[...] = before[...]
        for at in range(states.shape[0]):
            observe(at, jnp.broadcast_to(before[at : at + 1, :], parts.shape[1:]))

    share = own_states.shape[1]
    start = pl.multiple_of(lax.axis_index("state") * share, share)
    own_states[...] = states[:, pl.ds(start, share)]
    predicted[...] = readings[...].T[: states.shape[0], :]


def hop_pairs(turn, blocks):
    if 1 < turn < blocks - 1:
        return [(i, (i + 1) % blocks) for i in range(blocks)]
    rest = [i for i in range(blocks) if i not in (turn - 1, turn)]
    pairs = [(turn - 1, turn), (turn, turn - 1)]
    for i, j in zip(rest[::2], rest[1::2]):
        pairs += [(i, j), (j, i)]
    return pairs + [(i, i) for i in rest[len(rest) // 2 * 2 :]]


def per_device(
    observations, observed, loadings, noise_precision, blend_matrix, latent_rates, pair_latent,
    initial_mean,
):
    steps, outs, width = loadings.shape
    blocks = lax.axis_size("tm")
    share = width // lax.axis_size("state")
    other = functools.partial(lax.ppermute, axis_name="outputs", perm=[(0, 1), (1, 0)])
    in_hbm = functools.partial(
        pltpu.with_memory_space_constraint, memory_space=pltpu.HBM
    )
    loadings = in_hbm(loadings)
    sizes = part_sizes(steps)
    count = len(sizes)
    firsts = [sum(sizes[:i]) for i in range(count)]

    half = 2 * 3 * outs * width * width
    vector, gain_type = kept(8, width), kept(width, width, dtype=BF16)
    sems = pltpu.SemaphoreType.DMA

    def matrices(size):
        return kept(size, outs + 8, width)

    def chunk(size):
        return [kept(size, outs, width), matrices(size), matrices(size)]

    small = (steps, outs)
    *first_chunk, columns = call(
        stage_kernel,
        "stage",
        chunk(sizes[0]) + [kept(outs, 128)],
        [FAR] * 4,
        [
            pltpu.VMEM(small, observed.dtype),
            pltpu.VMEM(small, F32),
            pltpu.VMEM((1, outs), F32),
            pltpu.VMEM((128, outs), F32),
            sems((sizes[0],)),
            sems((3,)),
        ],
        moved=8 * sizes[0] * outs * width,
    )(loadings, in_hbm(observed), in_hbm(observations), in_hbm(noise_precision[None, :]))
    *second_chunk, parts, gain_high, gain_low, initial = call(
        functools.partial(second_kernel, firsts[1], steps),
        "second_part",
        chunk(sizes[1]) + [kept(2, 8, width), gain_type, gain_type, vector],
        [FAR] + [WHOLE] * 5,
        [sems((sizes[1],))],
        moved=8 * sizes[1] * outs * width,
    )(
        loadings, columns, latent_rates[None, :], pair_latent[None, :], blend_matrix,
        initial_mean[None, :],
    )
    gained_first, *later = call(
        functools.partial(third_kernel, firsts[2:], steps),
        "later_parts",
        [matrices(sizes[0])] + sum([chunk(size) for size in sizes[2:]], []),
        [FAR] + [WHOLE] * 4,
        [sems((size,)) for size in sizes[2:]],
        flops=sizes[0] * half,
        moved=8 * sum(sizes[2:]) * outs * width,
    )(loadings, columns, first_chunk[1], gain_high, gain_low)
    chunks = [first_chunk, second_chunk] + [later[i : i + 3] for i in range(0, len(later), 3)]
    loads_own, scaled_own, sent = zip(*chunks)
    gained_own = [gained_first] + list(
        call(
            functools.partial(gain_kernel, firsts[1:], steps),
            "own_gains",
            [matrices(size) for size in sizes[1:]],
            [WHOLE] * (1 + count),
            flops=sum(sizes[1:]) * half,
        )(gain_high, gain_low, *scaled_own[1:])
    )

    leaving = initial
    scaled, states, early = [], [], []
    for i in range(count):
        rows, state, leaving, *gained = call(
            functools.partial(part_kernel, i == 0, steps),
            "other_part",
            [matrices(sizes[i]), kept(sizes[i], width), vector]
            + ([matrices(sizes[i])] if i == 0 else []),
            [WHOLE, FAR] + [WHOLE] * 5,
            [sems],
            flops=sizes[i] * half // 3,
            moved=8 * sizes[i] * outs * width,
        )(
            leaving, other(sent[i]), scaled_own[i], parts, blend_matrix, gain_high, gain_low
        )
        scaled.append(rows)
        states.append(state)
        early += gained
    states = jnp.concatenate(states, axis=0)
    gained = call(
        functools.partial(late_kernel, firsts, steps),
        "late_gains",
        [matrices(size) for size in sizes],
        [FAR] + [WHOLE] * (2 + count),
        flops=steps * half,
    )(leaving, gain_high, gain_low, *scaled)
    operands = [*early]
    for group in zip(loads_own, scaled_own, gained_own, scaled, gained):
        operands += group

    specs = [WHOLE] * (4 + len(operands))
    entering = leaving
    for turn in range(1, blocks):
        entering = lax.ppermute(leaving, "tm", hop_pairs(turn, blocks))
        if turn < blocks - 1:
            states, leaving = call(
                functools.partial(block_kernel, turn, count),
                "block_chain",
                [kept(steps, width), vector],
                specs,
                flops=steps * half,
            )(states, entering, parts, blend_matrix, *operands)
    return tuple(
        call(
            functools.partial(last_kernel, blocks - 1 if blocks > 1 else -1, count),
            "last_chain",
            [
                jax.ShapeDtypeStruct((steps, share), F32),
                jax.ShapeDtypeStruct((steps, outs), F32),
            ],
            specs,
            [pltpu.VMEM((steps, width), F32), pltpu.VMEM((outs, 128), F32)],
            flops=steps * half,
        )(states, entering, parts, blend_matrix, *operands)
    )


def solution(mesh):
    placed = (
        P("tm", "outputs"),
        P("tm", "outputs"),
        P("tm", "outputs", None),
        P("outputs"),
        P(),
        P(),
        P(),
        P(),
    )
    return jax.shard_map(
        per_device,
        mesh=mesh,
        in_specs=placed,
        out_specs=(P("tm", "state"), P("tm", "outputs")),
        check_vma=False,
    )
```

```python
import functools

import jax
import jax.numpy as jnp
from jax import lax
from jax.experimental import pallas as pl
from jax.experimental.pallas import tpu as pltpu
from jax.sharding import PartitionSpec as P

F32, BF16 = jnp.float32, jnp.bfloat16
VMEM_LIMIT = 8 * 2**20
LAST_PART = 1
PARTS = 4
GAIN_STEPS = (0, 7, 9)
EARLY_STEPS = (0, 2, 2, 0)
WHOLE = pl.BlockSpec(memory_space=pltpu.VMEM)
FAR = pl.BlockSpec(memory_space=pl.ANY)


def call(kernel, name, outs, in_specs, scratch=(), flops=0, moved=0):
    return pl.pallas_call(
        kernel,
        out_shape=outs,
        in_specs=in_specs,
        out_specs=[WHOLE] * len(outs),
        scratch_shapes=scratch,
        compiler_params=pltpu.CompilerParams(vmem_limit_bytes=VMEM_LIMIT),
        cost_estimate=pl.CostEstimate(flops=flops, bytes_accessed=moved, transcendentals=0),
        name=name,
    )


def kept(*shape, dtype=F32):
    return pltpu.VMEM(shape, dtype)


def swap_pairs(x):
    width = x.shape[-1]
    lane = lax.broadcasted_iota(jnp.int32, x.shape, 1)
    return jnp.where(lane % 2 == 0, pltpu.roll(x, width - 1, 1), pltpu.roll(x, 1, 1))


def halves(x):
    high = x.astype(BF16)
    return high, (x - high.astype(F32)).astype(BF16)


def times_gain(scaled, gain_high, gain_low):
    high, low = halves(scaled)
    dot = functools.partial(jnp.dot, preferred_element_type=F32)
    return dot(high, gain_high) + (dot(high, gain_low) + dot(low, gain_high))


def part_sizes(steps):
    rest = steps - LAST_PART
    sizes = [(rest + PARTS - 2 - i) // (PARTS - 1) for i in range(PARTS - 1)]
    return sizes + [LAST_PART]


def copied(source, target, sem):
    copy = pltpu.make_async_copy(source, target, sem)
    copy.start()
    return copy


def fetched(loads_far, first, loads, sems):
    return [
        copied(loads_far.at[first + k], loads.at[k], sems.at[k]) for k in range(loads.shape[0])
    ]


def split(ref, size):
    outs = (ref.shape[0] - 8) // size
    return [
        (ref.at[pl.ds(k * outs, outs), :], ref.at[pl.ds(size * outs + k, 1), :])
        for k in range(size)
    ]


def scale(copies, first, steps, loads, columns, scaled, sent):
    size = loads.shape[0]
    targets = list(zip(split(scaled, size), split(sent, size)))
    for k, copy in enumerate(copies):
        at = first + k
        copy.wait()
        rows = loads[k] * columns[:, at : at + 1]
        tail = jnp.sum(columns[:, steps + at : steps + at + 1] * rows, axis=0, keepdims=True)
        for target, target_tail in targets[k]:
            target[...] = rows
            target_tail[...] = tail


def stage_kernel(
    loads_far, observed_far, observations_far, noise_far, loads, scaled, sent, columns,
    observed, observations, noise, turned, sems, small_sems,
):
    small = [
        copied(source, target, small_sems.at[i])
        for i, (source, target) in enumerate(
            (
                (observed_far, observed),
                (observations_far, observations),
                (noise_far, noise),
            )
        )
    ]
    copies = fetched(loads_far, 0, loads, sems)
    turned[...] = jnp.zeros_like(turned)
    for copy in small:
        copy.wait()
    steps = observed.shape[0]
    root = jnp.sqrt(observed[...].astype(F32) * noise[...])
    turned[:steps, :] = root
    turned[steps : 2 * steps, :] = root * observations[...]
    columns[:, : turned.shape[0]] = turned[...].T
    scale(copies, 0, steps, loads, columns, scaled, sent)


def transition(rates, pairs, width):
    layout = pairs[...]
    rate = jnp.zeros(layout.shape, F32)
    for latent in range(rates.shape[1]):
        rate = jnp.where(layout == latent, rates[:, latent : latent + 1], rate)
    spread = lax.broadcasted_iota(jnp.int32, (layout.shape[1], width), 1) // 2
    spread = spread == lax.broadcasted_iota(jnp.int32, spread.shape, 0)
    rate = jnp.dot(
        jnp.broadcast_to(rate, (8, layout.shape[1])),
        spread.astype(F32),
        precision=lax.Precision.HIGHEST,
        preferred_element_type=F32,
    )
    even = lax.broadcasted_iota(jnp.int32, rate.shape, 1) % 2 == 0
    damping = jnp.exp(-rate)
    diagonal = jnp.where(even, damping * (1.0 + rate), damping * (1.0 - rate))
    cross = jnp.where(even, damping, -damping * rate * rate)
    return diagonal, cross


def gain_limit(block, steps):
    return min(GAIN_STEPS[block], steps) if block < len(GAIN_STEPS) else steps


def early_limit(block, size):
    return min(EARLY_STEPS[min(block, len(EARLY_STEPS) - 1)], size)


def by_block(work, steps):
    block = lax.axis_index("tm")
    kinds = min(len(GAIN_STEPS), lax.axis_size("tm") - 1)
    for i in range(1, kinds + 1):

        @pl.when(block == i if i < kinds else block >= i)
        def _():
            work(i, gain_limit(i, steps))


def fill_gains(limit, first, size, scaled, gain_high, gain_low, gained, begin=0):
    tails = scaled[scaled.shape[0] - 8 :, :]
    sources, targets = split(scaled, size), split(gained, size)
    for k in range(begin, min(size, limit - first)):
        rows = jnp.concatenate([sources[k][0][...], tails, tails], axis=0)
        rows = times_gain(rows, gain_high[...], gain_low[...])
        outs = rows.shape[0] - 16
        targets[k][0][...] = rows[:outs]
        targets[k][1][...] = rows[outs + k : outs + k + 1]


def rest_kernel(
    firsts, steps, loads_far, columns, rates, pairs, blend, mean,
    parts, gain_high, gain_low, initial, *rest,
):
    count = len(firsts)
    groups = [rest[3 * i : 3 * i + 3] for i in range(count)]
    sems = rest[3 * count :]
    copies = [
        fetched(loads_far, first, group[0], sem)
        for first, group, sem in zip(firsts, groups, sems)
    ]
    diagonal, cross = transition(rates, pairs, blend.shape[1])
    parts[0] = diagonal
    parts[1] = cross
    initial[...] = jnp.broadcast_to(mean[...], initial.shape)

    @pl.when(lax.axis_index("tm") != 0)
    def _():
        gain = blend[...]
        gain = gain * diagonal[0:1] + swap_pairs(gain) * cross[0:1]
        gain_high[...], gain_low[...] = halves(gain)

    for first, group, copy in zip(firsts, groups, copies):
        loads, scaled, sent = group
        scale(copy, first, steps, loads, columns, scaled, sent)


def gain_kernel(firsts, sizes, steps, gain_high, gain_low, *rest):
    count = len(firsts)

    def work(block, limit):
        for first, size, scaled, gained in zip(firsts, sizes, rest[:count], rest[count:]):
            fill_gains(limit, first, size, scaled, gain_high, gain_low, gained)

    by_block(work, steps)


def reflected(state, pull, blend):
    pull = jnp.broadcast_to(pull, state.shape)
    place = lax.broadcasted_iota(jnp.int32, (8, 128), 1) - lax.broadcasted_iota(
        jnp.int32, (8, 128), 0
    )
    turned = []
    for start in range(0, state.shape[1], 128):
        total = jnp.zeros((8, 128), F32)
        for row in range(0, 128, 8):
            blended = blend[start + row : start + row + 8, :] * pull
            total = total + jnp.where(
                place == row, jnp.sum(blended, axis=1, keepdims=True), 0.0
            )
        turned.append(jnp.sum(total, axis=0, keepdims=True))
    return state - jnp.concatenate(turned, axis=1)


def advance(state, scaled, gained, parts, blend=None):
    pull = 0.0
    for (rows, _), (gains, shift) in zip(scaled, gained):
        total = jnp.zeros_like(state)
        for row in range(0, rows.shape[0], 8):
            block = rows[row : row + 8, :]
            reading = jnp.sum(block * state, axis=1, keepdims=True)
            total = total + reading * (block if blend is not None else gains[row : row + 8, :])
        pull += jnp.sum(total, axis=0, keepdims=True) - shift[...]
    if blend is not None:
        state, pull = reflected(state, pull, blend), 0.0
    return state * parts[0] + swap_pairs(state) * parts[1] - pull


def part_kernel(
    early, size, steps, entering, arrived, scaled_own, parts, blend, gain_high, gain_low,
    scaled, states, leaving, *rest,
):
    *gained, sem = rest
    block = lax.axis_index("tm")

    @pl.when(block == 0)
    def _():
        state = jnp.broadcast_to(entering[0:1, :], parts.shape[1:])
        for k, pair in enumerate(zip(split(scaled_own, size), split(arrived, size))):
            state = advance(state, pair, pair, parts, blend)
            states[k : k + 1, :] = state[0:1, :]
        leaving[...] = state

    @pl.when(block != 0)
    def _():
        copied(arrived, scaled, sem).wait()

    def work(block, limit):
        limit = early_limit(block, size)
        fill_gains(limit, 0, size, arrived, gain_high, gain_low, *gained)

    if early:
        by_block(work, steps)


def late_kernel(firsts, sizes, steps, _, gain_high, gain_low, *rest):
    count = len(firsts)
    parts = list(zip(firsts, sizes, rest[:count], rest[count:]))

    def work(block, limit):
        for i, (first, size, scaled, gained) in enumerate(parts):
            begin = 0 if i else early_limit(block, size)
            fill_gains(limit, first, size, scaled, gain_high, gain_low, gained, begin)

    by_block(work, steps)


def chain(turn, entering, parts, blend, operands, early, states, observe=None):
    limit = gain_limit(turn, states.shape[0])
    state = jnp.broadcast_to(entering[0:1, :], parts.shape[1:])
    at = 0
    for loads, *refs in operands:
        size = loads.shape[0]
        early_gains = split(early, size) if at == 0 else []
        for k, (own, gained_own, other, gained) in enumerate(
            zip(*[split(ref, size) for ref in refs])
        ):
            pair = (own, other)
            if at < limit:
                if at < early_limit(turn, len(early_gains)):
                    gained = early_gains[k]
                state = advance(state, pair, (gained_own, gained), parts)
            else:
                state = advance(state, pair, pair, parts, blend)
            states[at : at + 1, :] = state[0:1, :]
            if observe is not None:
                observe(at, state)
            at += 1
    return state


def grouped(refs, count):
    return [refs[5 * i : 5 * i + 5] for i in range(count)], refs[5 * count :]


def block_kernel(turn, count, before, entering, parts, blend, early, *refs):
    operands, (states, leaving) = grouped(refs, count)
    block = lax.axis_index("tm")

    @pl.when(block == turn)
    def _():
        leaving[...] = chain(turn, entering, parts, blend, operands, early, states)

    @pl.when(block != turn)
    def _():
        states[...] = before[...]
        leaving[...] = jnp.zeros_like(leaving)


def observation(operands, readings):
    rows = [loads.at[k] for loads, *_ in operands for k in range(loads.shape[0])]

    def observe(at, state):
        outs = rows[at].shape[0]
        for row in range(0, outs, 8):
            product = rows[at][row : row + 8, :] * state
            readings[row : row + 8, at : at + 1] = jnp.sum(product, axis=1, keepdims=True)

    return observe


def report(states, readings, own_states, predicted):
    share = own_states.shape[1]
    start = pl.multiple_of(lax.axis_index("state") * share, share)
    own_states[...] = states[:, pl.ds(start, share)]
    predicted[...] = readings[...].T[: states.shape[0], :]


def finished_kernel(turn, count, states, *refs):
    loads, (own_states, predicted, readings) = refs[:count], refs[count:]

    @pl.when(lax.axis_index("tm") != turn)
    def _():
        observe = observation([(load,) for load in loads], readings)
        for at in range(states.shape[0]):
            observe(at, jnp.broadcast_to(states[at : at + 1, :], (8, states.shape[1])))
        report(states, readings, own_states, predicted)


def last_kernel(turn, count, ready_states, ready, entering, parts, blend, early, *refs):
    operands, (own_states, predicted, states, readings) = grouped(refs, count)
    block = lax.axis_index("tm")

    @pl.when(block == turn)
    def _():
        observe = observation(operands, readings)
        chain(turn, entering, parts, blend, operands, early, states, observe)
        report(states, readings, own_states, predicted)

    @pl.when(block != turn)
    def _():
        own_states[...] = ready_states[...]
        predicted[...] = ready[...]


def hop_pairs(turn, blocks):
    if 1 < turn < blocks - 1:
        return [(i, (i + 1) % blocks) for i in range(blocks)]
    rest = [i for i in range(blocks) if i not in (turn - 1, turn)]
    pairs = [(turn - 1, turn), (turn, turn - 1)]
    for i, j in zip(rest[::2], rest[1::2]):
        pairs += [(i, j), (j, i)]
    return pairs + [(i, i) for i in rest[len(rest) // 2 * 2 :]]


def per_device(
    observations, observed, loadings, noise_precision, blend_matrix, latent_rates, pair_latent,
    initial_mean,
):
    steps, outs, width = loadings.shape
    blocks = lax.axis_size("tm")
    share = width // lax.axis_size("state")
    other = functools.partial(lax.ppermute, axis_name="outputs", perm=[(0, 1), (1, 0)])
    in_hbm = functools.partial(
        pltpu.with_memory_space_constraint, memory_space=pltpu.HBM
    )
    loadings = in_hbm(loadings)
    sizes = part_sizes(steps)
    count = len(sizes)
    firsts = [sum(sizes[:i]) for i in range(count)]

    half = 2 * 3 * outs * width * width
    vector, gain_type = kept(8, width), kept(width, width, dtype=BF16)
    sems = pltpu.SemaphoreType.DMA

    def matrices(size):
        return kept(size * outs + 8, width)

    def chunk(size):
        return [kept(size, outs, width), matrices(size), matrices(size)]

    small = (steps, outs)
    *first_chunk, columns = call(
        stage_kernel,
        "stage",
        chunk(sizes[0]) + [kept(outs, 128)],
        [FAR] * 4,
        [
            pltpu.VMEM(small, observed.dtype),
            pltpu.VMEM(small, F32),
            pltpu.VMEM((1, outs), F32),
            pltpu.VMEM((-(-2 * steps // 8) * 8, outs), F32),
            sems((sizes[0],)),
            sems((3,)),
        ],
        moved=8 * sizes[0] * outs * width,
    )(loadings, in_hbm(observed), in_hbm(observations), in_hbm(noise_precision[None, :]))
    parts, gain_high, gain_low, initial, *later = call(
        functools.partial(rest_kernel, firsts[1:], steps),
        "rest",
        [kept(2, 8, width), gain_type, gain_type, vector]
        + sum([chunk(size) for size in sizes[1:]], []),
        [FAR] + [WHOLE] * 5,
        [sems((size,)) for size in sizes[1:]],
        moved=8 * sum(sizes[1:]) * outs * width,
    )(
        loadings, columns, latent_rates[None, :], pair_latent[None, :], blend_matrix,
        initial_mean[None, :],
    )
    chunks = [first_chunk] + [later[i : i + 3] for i in range(0, len(later), 3)]
    loads_own, scaled_own, sent = zip(*chunks)
    gained_own = call(
        functools.partial(gain_kernel, firsts, sizes, steps),
        "own_gains",
        [matrices(size) for size in sizes],
        [WHOLE] * (2 + count),
        flops=steps * half,
    )(gain_high, gain_low, *scaled_own)

    leaving = initial
    scaled, states, early = [], [], []
    for i in range(count):
        rows, state, leaving, *gained = call(
            functools.partial(part_kernel, i == 0, sizes[i], steps),
            "other_part",
            [matrices(sizes[i]), kept(sizes[i], width), vector]
            + ([matrices(sizes[i])] if i == 0 else []),
            [WHOLE] * 7,
            [sems],
            flops=sizes[i] * half // 3,
            moved=8 * sizes[i] * outs * width,
        )(
            leaving, other(sent[i]), scaled_own[i], parts, blend_matrix, gain_high, gain_low
        )
        scaled.append(rows)
        states.append(state)
        early += gained
    states = jnp.concatenate(states, axis=0)
    gained = call(
        functools.partial(late_kernel, firsts, sizes, steps),
        "late_gains",
        [matrices(size) for size in sizes],
        [FAR] + [WHOLE] * (2 + count),
        flops=steps * half,
    )(leaving, gain_high, gain_low, *scaled)
    operands = [*early]
    for group in zip(loads_own, scaled_own, gained_own, scaled, gained):
        operands += group

    specs = [WHOLE] * (4 + len(operands))
    entering = leaving
    for turn in range(1, blocks):
        entering = lax.ppermute(leaving, "tm", hop_pairs(turn, blocks))
        if turn < blocks - 1:
            states, leaving = call(
                functools.partial(block_kernel, turn, count),
                "block_chain",
                [kept(steps, width), vector],
                specs,
                flops=steps * half,
            )(states, entering, parts, blend_matrix, *operands)
    last = blocks - 1 if blocks > 1 else -1
    ready = call(
        functools.partial(finished_kernel, last, count),
        "finished",
        [kept(steps, share), kept(steps, outs)],
        [WHOLE] * (1 + count),
        [pltpu.VMEM((outs, 128), F32)],
        flops=steps * half,
    )(states, *loads_own)
    return tuple(
        call(
            functools.partial(last_kernel, last, count),
            "last_chain",
            [
                jax.ShapeDtypeStruct((steps, share), F32),
                jax.ShapeDtypeStruct((steps, outs), F32),
            ],
            [WHOLE] * (5 + len(operands)),
            [pltpu.VMEM((steps, width), F32), pltpu.VMEM((outs, 128), F32)],
            flops=steps * half,
        )(*ready, entering, parts, blend_matrix, *operands)
    )


def solution(mesh):
    placed = (
        P("tm", "outputs"),
        P("tm", "outputs"),
        P("tm", "outputs", None),
        P("outputs"),
        P(),
        P(),
        P(),
        P(),
    )
    return jax.shard_map(
        per_device,
        mesh=mesh,
        in_specs=placed,
        out_specs=(P("tm", "state"), P("tm", "outputs")),
        check_vma=False,
    )
```

```python
import functools

import jax
import jax.numpy as jnp
from jax import lax
from jax.experimental import pallas as pl
from jax.experimental.pallas import tpu as pltpu
from jax.sharding import PartitionSpec as P

F32, BF16 = jnp.float32, jnp.bfloat16
VMEM_LIMIT = 8 * 2**20
LAST_PART = 1
PARTS = 4
GAIN_STEPS = (0, 8, 10)
EARLY_STEPS = (0, 4, 2, 0)
WHOLE = pl.BlockSpec(memory_space=pltpu.VMEM)
FAR = pl.BlockSpec(memory_space=pl.ANY)


def call(kernel, name, outs, in_specs, scratch=(), flops=0, moved=0, out_spec=WHOLE, aliases=()):
    return pl.pallas_call(
        kernel,
        out_shape=outs,
        in_specs=in_specs,
        out_specs=[out_spec] * len(outs),
        input_output_aliases=dict(aliases),
        scratch_shapes=scratch,
        compiler_params=pltpu.CompilerParams(vmem_limit_bytes=VMEM_LIMIT),
        cost_estimate=pl.CostEstimate(flops=flops, bytes_accessed=moved, transcendentals=0),
        name=name,
    )


def kept(*shape, dtype=F32):
    return pltpu.VMEM(shape, dtype)


def swap_pairs(x):
    width = x.shape[-1]
    lane = lax.broadcasted_iota(jnp.int32, x.shape, 1)
    return jnp.where(lane % 2 == 0, pltpu.roll(x, width - 1, 1), pltpu.roll(x, 1, 1))


def halves(x):
    high = x.astype(BF16)
    return high, (x - high.astype(F32)).astype(BF16)


def times_gain(scaled, gain_high, gain_low):
    high, low = halves(scaled)
    dot = functools.partial(jnp.dot, preferred_element_type=F32)
    return dot(high, gain_high) + (dot(high, gain_low) + dot(low, gain_high))


def part_sizes(steps):
    rest = steps - LAST_PART
    sizes = [(rest + PARTS - 2 - i) // (PARTS - 1) for i in range(PARTS - 1)]
    return sizes + [LAST_PART]


def copied(source, target, sem):
    copy = pltpu.make_async_copy(source, target, sem)
    copy.start()
    return copy


def fetched(loads_far, first, loads, sems):
    return [
        copied(loads_far.at[first + k], loads.at[k], sems.at[k]) for k in range(loads.shape[0])
    ]


def split(ref, size):
    outs = (ref.shape[0] - 8) // size
    return [
        (ref.at[pl.ds(k * outs, outs), :], ref.at[pl.ds(size * outs + k, 1), :])
        for k in range(size)
    ]


def scale(copies, first, steps, loads, columns, scaled, sent):
    size = loads.shape[0]
    targets = list(zip(split(scaled, size), split(sent, size)))
    for k, copy in enumerate(copies):
        at = first + k
        copy.wait()
        rows = loads[k] * columns[:, at : at + 1]
        tail = jnp.sum(columns[:, steps + at : steps + at + 1] * rows, axis=0, keepdims=True)
        for target, target_tail in targets[k]:
            target[...] = rows
            target_tail[...] = tail


def stage_kernel(
    loads_far, observed_far, observations_far, noise_far, loads, scaled, sent, columns,
    observed, observations, noise, turned, sems, small_sems,
):
    small = [
        copied(source, target, small_sems.at[i])
        for i, (source, target) in enumerate(
            (
                (observed_far, observed),
                (observations_far, observations),
                (noise_far, noise),
            )
        )
    ]
    copies = fetched(loads_far, 0, loads, sems)
    turned[...] = jnp.zeros_like(turned)
    for copy in small:
        copy.wait()
    steps = observed.shape[0]
    root = jnp.sqrt(observed[...].astype(F32) * noise[...])
    turned[:steps, :] = root
    turned[steps : 2 * steps, :] = root * observations[...]
    columns[:, : turned.shape[0]] = turned[...].T
    scale(copies, 0, steps, loads, columns, scaled, sent)


def transition(rates, pairs, width):
    layout = pairs[...]
    rate = jnp.zeros(layout.shape, F32)
    for latent in range(rates.shape[1]):
        rate = jnp.where(layout == latent, rates[:, latent : latent + 1], rate)
    spread = lax.broadcasted_iota(jnp.int32, (layout.shape[1], width), 1) // 2
    spread = spread == lax.broadcasted_iota(jnp.int32, spread.shape, 0)
    rate = jnp.dot(
        jnp.broadcast_to(rate, (8, layout.shape[1])),
        spread.astype(F32),
        precision=lax.Precision.HIGHEST,
        preferred_element_type=F32,
    )
    even = lax.broadcasted_iota(jnp.int32, rate.shape, 1) % 2 == 0
    damping = jnp.exp(-rate)
    diagonal = jnp.where(even, damping * (1.0 + rate), damping * (1.0 - rate))
    cross = jnp.where(even, damping, -damping * rate * rate)
    return diagonal, cross


def gain_limit(block, steps):
    return min(GAIN_STEPS[block], steps) if block < len(GAIN_STEPS) else steps


def early_limit(block, size):
    return min(EARLY_STEPS[min(block, len(EARLY_STEPS) - 1)], size)


def by_block(work, steps):
    block = lax.axis_index("tm")
    kinds = min(len(GAIN_STEPS), lax.axis_size("tm") - 1)
    for i in range(1, kinds + 1):

        @pl.when(block == i if i < kinds else block >= i)
        def _():
            work(i, gain_limit(i, steps))


def fill_gains(limit, first, size, scaled, gain_high, gain_low, gained, begin=0):
    sources, targets = split(scaled, size), split(gained, size)
    end = min(size, limit - first)
    for k in range(begin, end):
        rows = sources[k][0][...]
        outs = rows.shape[0]
        if k == begin:
            tails = scaled[scaled.shape[0] - 8 :, :]
            rows = jnp.concatenate([rows, tails, tails], axis=0)
        rows = times_gain(rows, gain_high[...], gain_low[...])
        targets[k][0][...] = rows[:outs]
        if k == begin:
            for j in range(begin, end):
                targets[j][1][...] = rows[outs + j : outs + j + 1]


def rest_kernel(
    firsts, steps, loads_far, columns, rates, pairs, blend, mean,
    parts, gain_high, gain_low, initial, *rest,
):
    count = len(firsts)
    groups = [rest[3 * i : 3 * i + 3] for i in range(count)]
    sems = rest[3 * count :]
    copies = [
        fetched(loads_far, first, group[0], sem)
        for first, group, sem in zip(firsts, groups, sems)
    ]
    diagonal, cross = transition(rates, pairs, blend.shape[1])
    parts[0] = diagonal
    parts[1] = cross
    initial[...] = jnp.broadcast_to(mean[...], initial.shape)

    @pl.when(lax.axis_index("tm") != 0)
    def _():
        gain = blend[...]
        gain = gain * diagonal[0:1] + swap_pairs(gain) * cross[0:1]
        gain_high[...], gain_low[...] = halves(gain)

    for first, group, copy in zip(firsts, groups, copies):
        loads, scaled, sent = group
        scale(copy, first, steps, loads, columns, scaled, sent)


def gain_kernel(firsts, sizes, steps, gain_high, gain_low, *rest):
    count = len(firsts)

    def work(block, limit):
        for first, size, scaled, gained in zip(firsts, sizes, rest[:count], rest[count:]):
            fill_gains(limit, first, size, scaled, gain_high, gain_low, gained)

    by_block(work, steps)


def reflected(state, pull, blend):
    pull = jnp.broadcast_to(pull, state.shape)
    place = lax.broadcasted_iota(jnp.int32, (8, 128), 1) - lax.broadcasted_iota(
        jnp.int32, (8, 128), 0
    )
    turned = []
    for start in range(0, state.shape[1], 128):
        totals = [jnp.zeros((8, 128), F32) for _ in range(2)]
        for row in range(0, 128, 8):
            blended = blend[start + row : start + row + 8, :] * pull
            i = row // 8 % len(totals)
            totals[i] = totals[i] + jnp.where(
                place == row, jnp.sum(blended, axis=1, keepdims=True), 0.0
            )
        turned.append(jnp.sum(sum(totals[1:], totals[0]), axis=0, keepdims=True))
    return state - jnp.concatenate(turned, axis=1)


def advance(state, scaled, gained, parts, blend=None, beside=None):
    sides = []
    for (rows, _), (gains, _) in zip(scaled, gained):
        totals = [jnp.zeros_like(state), jnp.zeros_like(state)]
        for row in range(0, rows.shape[0], 8):
            block = rows[row : row + 8, :]
            reading = jnp.sum(block * state, axis=1, keepdims=True)
            if blend is None:
                block = gains[row : row + 8, :]
            totals[row // 8 % 2] = totals[row // 8 % 2] + reading * block
            if beside is not None and not sides:
                beside(row)
        sides.append(totals[0] + totals[1])
    pull = jnp.sum(sides[0] + sides[1], axis=0, keepdims=True)
    pull = pull - (gained[0][1][...] + gained[1][1][...])
    if blend is not None:
        state, pull = reflected(state, pull, blend), 0.0
    return state * parts[0] + swap_pairs(state) * parts[1] - pull


def part_kernel(
    early, size, steps, entering, arrived, scaled_own, parts, blend, gain_high, gain_low,
    scaled, states, leaving, *rest,
):
    *gained, sem = rest
    block = lax.axis_index("tm")

    @pl.when(block == 0)
    def _():
        state = jnp.broadcast_to(entering[0:1, :], parts.shape[1:])
        for k, pair in enumerate(zip(split(scaled_own, size), split(arrived, size))):
            state = advance(state, pair, pair, parts, blend)
            states[k : k + 1, :] = state[0:1, :]
        leaving[...] = state

    @pl.when(block != 0)
    def _():
        copied(arrived, scaled, sem).wait()

    def work(block, limit):
        limit = early_limit(block, size)
        fill_gains(limit, 0, size, arrived, gain_high, gain_low, *gained)

    if early:
        by_block(work, steps)


def late_kernel(firsts, sizes, steps, _, gain_high, gain_low, *rest):
    count = len(firsts)
    parts = list(zip(firsts, sizes, rest[:count], rest[count:]))

    def work(block, limit):
        for i, (first, size, scaled, gained) in enumerate(parts):
            begin = 0 if i else early_limit(block, size)
            fill_gains(limit, first, size, scaled, gain_high, gain_low, gained, begin)

    by_block(work, steps)


def chain(turn, entering, parts, blend, operands, early, states, observe=None):
    limit = gain_limit(turn, states.shape[0])
    state = jnp.broadcast_to(entering[0:1, :], parts.shape[1:])
    at = 0
    for loads, *refs in operands:
        size = loads.shape[0]
        early_gains = split(early, size) if at == 0 else []
        for k, (own, gained_own, other, gained) in enumerate(
            zip(*[split(ref, size) for ref in refs])
        ):
            pair = (own, other)
            beside = None
            if observe is not None and at > 0:
                beside = functools.partial(observe, at - 1, state)
            if at < limit:
                if at < early_limit(turn, len(early_gains)):
                    gained = early_gains[k]
                state = advance(state, pair, (gained_own, gained), parts, beside=beside)
            else:
                state = advance(state, pair, pair, parts, blend, beside)
            states[at : at + 1, :] = state[0:1, :]
            at += 1
    if observe is not None:
        for row in range(0, operands[0][0].shape[1], 8):
            observe(at - 1, state, row)
    return state


def grouped(refs, count):
    return [refs[5 * i : 5 * i + 5] for i in range(count)], refs[5 * count :]


def block_kernel(turn, count, before, entering, parts, blend, early, *refs):
    operands, (states, leaving) = grouped(refs, count)
    block = lax.axis_index("tm")

    @pl.when(block == turn)
    def _():
        leaving[...] = chain(turn, entering, parts, blend, operands, early, states)

    @pl.when(block != turn)
    def _():
        states[...] = before[...]
        leaving[...] = jnp.zeros_like(leaving)


def observation(operands, predicted):
    rows = [loads.at[k] for loads, *_ in operands for k in range(loads.shape[0])]
    place = lax.broadcasted_iota(jnp.int32, (8, 128), 1) - lax.broadcasted_iota(
        jnp.int32, (8, 128), 0
    )
    outs = predicted.shape[1]
    totals = {}

    def observe(at, state, row):
        reading = jnp.sum(rows[at][row : row + 8, :] * state, axis=1, keepdims=True)
        kept_rows = jnp.where(place == row % 128, reading, 0.0)
        key = (at, row // 128)
        totals[key] = totals[key] + kept_rows if key in totals else kept_rows
        if row == outs - 8:
            for start in range(0, outs, 128):
                total = jnp.sum(totals[(at, start // 128)], axis=0, keepdims=True)
                predicted[at : at + 1, start : start + 128] = total

    return observe


def own_share(states, share):
    start = pl.multiple_of(lax.axis_index("state") * share, share)
    return states[:, pl.ds(start, share)]


def finished_kernel(turn, count, states, *refs):
    loads, (own_states, predicted) = refs[:count], refs[count:]

    @pl.when(lax.axis_index("tm") != turn)
    def _():
        observe = observation([(load,) for load in loads], predicted)
        for at in range(states.shape[0]):
            state = jnp.broadcast_to(states[at : at + 1, :], (8, states.shape[1]))
            for row in range(0, loads[0].shape[1], 8):
                observe(at, state, row)
        own_states[...] = own_share(states, own_states.shape[1])


def last_kernel(turn, count, ready_states, ready, entering, parts, blend, early, *refs):
    operands, rest = grouped(refs, count)
    own_far, predicted_far, own_states, predicted, states, sems = rest

    @pl.when(lax.axis_index("tm") == turn)
    def _():
        observe = observation(operands, predicted)
        chain(turn, entering, parts, blend, operands, early, states, observe)
        own_states[...] = own_share(states, own_states.shape[1])
        first = copied(own_states, own_far, sems.at[0])
        second = copied(predicted, predicted_far, sems.at[1])
        first.wait()
        second.wait()


def hop_pairs(turn, blocks):
    if 1 < turn < blocks - 1:
        return [(i, (i + 1) % blocks) for i in range(blocks)]
    rest = [i for i in range(blocks) if i not in (turn - 1, turn)]
    pairs = [(turn - 1, turn), (turn, turn - 1)]
    for i, j in zip(rest[::2], rest[1::2]):
        pairs += [(i, j), (j, i)]
    return pairs + [(i, i) for i in rest[len(rest) // 2 * 2 :]]


def per_device(
    observations, observed, loadings, noise_precision, blend_matrix, latent_rates, pair_latent,
    initial_mean,
):
    steps, outs, width = loadings.shape
    blocks = lax.axis_size("tm")
    share = width // lax.axis_size("state")
    other = functools.partial(lax.ppermute, axis_name="outputs", perm=[(0, 1), (1, 0)])
    in_hbm = functools.partial(
        pltpu.with_memory_space_constraint, memory_space=pltpu.HBM
    )
    loadings = in_hbm(loadings)
    sizes = part_sizes(steps)
    count = len(sizes)
    firsts = [sum(sizes[:i]) for i in range(count)]

    half = 2 * 3 * outs * width * width
    vector, gain_type = kept(8, width), kept(width, width, dtype=BF16)
    sems = pltpu.SemaphoreType.DMA

    def matrices(size):
        return kept(size * outs + 8, width)

    def chunk(size):
        return [kept(size, outs, width), matrices(size), matrices(size)]

    small = (steps, outs)
    *first_chunk, columns = call(
        stage_kernel,
        "stage",
        chunk(sizes[0]) + [kept(outs, 128)],
        [FAR] * 4,
        [
            pltpu.VMEM(small, observed.dtype),
            pltpu.VMEM(small, F32),
            pltpu.VMEM((1, outs), F32),
            pltpu.VMEM((-(-2 * steps // 8) * 8, outs), F32),
            sems((sizes[0],)),
            sems((3,)),
        ],
        moved=8 * sizes[0] * outs * width,
    )(loadings, in_hbm(observed), in_hbm(observations), in_hbm(noise_precision[None, :]))
    parts, gain_high, gain_low, initial, *later = call(
        functools.partial(rest_kernel, firsts[1:], steps),
        "rest",
        [kept(2, 8, width), gain_type, gain_type, vector]
        + sum([chunk(size) for size in sizes[1:]], []),
        [FAR] + [WHOLE] * 5,
        [sems((size,)) for size in sizes[1:]],
        moved=8 * sum(sizes[1:]) * outs * width,
    )(
        loadings, columns, latent_rates[None, :], pair_latent[None, :], blend_matrix,
        initial_mean[None, :],
    )
    chunks = [first_chunk] + [later[i : i + 3] for i in range(0, len(later), 3)]
    loads_own, scaled_own, sent = zip(*chunks)
    gained_own = call(
        functools.partial(gain_kernel, firsts, sizes, steps),
        "own_gains",
        [matrices(size) for size in sizes],
        [WHOLE] * (2 + count),
        flops=steps * half,
    )(gain_high, gain_low, *scaled_own)

    leaving = initial
    scaled, states, early = [], [], []
    for i in range(count):
        rows, state, leaving, *gained = call(
            functools.partial(part_kernel, i == 0, sizes[i], steps),
            "other_part",
            [matrices(sizes[i]), kept(sizes[i], width), vector]
            + ([matrices(sizes[i])] if i == 0 else []),
            [WHOLE] * 7,
            [sems],
            flops=sizes[i] * half // 3,
            moved=8 * sizes[i] * outs * width,
        )(
            leaving, other(sent[i]), scaled_own[i], parts, blend_matrix, gain_high, gain_low
        )
        scaled.append(rows)
        states.append(state)
        early += gained
    states = jnp.concatenate(states, axis=0)
    gained = call(
        functools.partial(late_kernel, firsts, sizes, steps),
        "late_gains",
        [matrices(size) for size in sizes],
        [FAR] + [WHOLE] * (2 + count),
        flops=steps * half,
    )(leaving, gain_high, gain_low, *scaled)
    operands = [*early]
    for group in zip(loads_own, scaled_own, gained_own, scaled, gained):
        operands += group

    specs = [WHOLE] * (4 + len(operands))
    entering = leaving
    for turn in range(1, blocks):
        entering = lax.ppermute(leaving, "tm", hop_pairs(turn, blocks))
        if turn < blocks - 1:
            states, leaving = call(
                functools.partial(block_kernel, turn, count),
                "block_chain",
                [kept(steps, width), vector],
                specs,
                flops=steps * half,
            )(states, entering, parts, blend_matrix, *operands)
    last = blocks - 1 if blocks > 1 else -1
    outputs = [
        jax.ShapeDtypeStruct((steps, share), F32),
        jax.ShapeDtypeStruct((steps, outs), F32),
    ]
    ready = call(
        functools.partial(finished_kernel, last, count),
        "finished",
        outputs,
        [WHOLE] * (1 + count),
        flops=steps * half,
    )(states, *loads_own)
    return tuple(
        call(
            functools.partial(last_kernel, last, count),
            "last_chain",
            outputs,
            [FAR] * 2 + [WHOLE] * (3 + len(operands)),
            [
                pltpu.VMEM((steps, share), F32),
                pltpu.VMEM((steps, outs), F32),
                pltpu.VMEM((steps, width), F32),
                sems((2,)),
            ],
            flops=steps * half,
            out_spec=FAR,
            aliases=((0, 0), (1, 1)),
        )(*ready, entering, parts, blend_matrix, *operands)
    )


def solution(mesh):
    placed = (
        P("tm", "outputs"),
        P("tm", "outputs"),
        P("tm", "outputs", None),
        P("outputs"),
        P(),
        P(),
        P(),
        P(),
    )
    return jax.shard_map(
        per_device,
        mesh=mesh,
        in_specs=placed,
        out_specs=(P("tm", "state"), P("tm", "outputs")),
        check_vma=False,
    )
```

```python
import functools

import jax
import jax.numpy as jnp
from jax import lax
from jax.experimental import pallas as pl
from jax.experimental.pallas import tpu as pltpu
from jax.sharding import PartitionSpec as P

F32, BF16 = jnp.float32, jnp.bfloat16
VMEM_LIMIT = 8 * 2**20
LAST_PART = 1
PARTS = 4
GAIN_STEPS = (0, 8, 10)
EARLY_STEPS = (0, 4, 3, 0)
WHOLE = pl.BlockSpec(memory_space=pltpu.VMEM)
FAR = pl.BlockSpec(memory_space=pl.ANY)


def call(kernel, name, outs, in_specs, scratch=(), flops=0, moved=0, out_spec=WHOLE, aliases=()):
    return pl.pallas_call(
        kernel,
        out_shape=outs,
        in_specs=in_specs,
        out_specs=[out_spec] * len(outs),
        input_output_aliases=dict(aliases),
        scratch_shapes=scratch,
        compiler_params=pltpu.CompilerParams(vmem_limit_bytes=VMEM_LIMIT),
        cost_estimate=pl.CostEstimate(flops=flops, bytes_accessed=moved, transcendentals=0),
        name=name,
    )


def kept(*shape, dtype=F32):
    return pltpu.VMEM(shape, dtype)


def swap_pairs(x):
    width = x.shape[-1]
    lane = lax.broadcasted_iota(jnp.int32, x.shape, 1)
    return jnp.where(lane % 2 == 0, pltpu.roll(x, width - 1, 1), pltpu.roll(x, 1, 1))


def halves(x):
    high = x.astype(BF16)
    return high, (x - high.astype(F32)).astype(BF16)


def times_gain(scaled, gain_high, gain_low):
    high, low = halves(scaled)
    dot = functools.partial(jnp.dot, preferred_element_type=F32)
    return dot(high, gain_high) + (dot(high, gain_low) + dot(low, gain_high))


def part_sizes(steps):
    rest = steps - LAST_PART
    sizes = [(rest + PARTS - 2 - i) // (PARTS - 1) for i in range(PARTS - 1)]
    return sizes + [LAST_PART]


def copied(source, target, sem):
    copy = pltpu.make_async_copy(source, target, sem)
    copy.start()
    return copy


def fetched(loads_far, first, loads, sems):
    return [
        copied(loads_far.at[first + k], loads.at[k], sems.at[k]) for k in range(loads.shape[0])
    ]


def split(ref, size):
    outs = (ref.shape[0] - 8) // size
    return [
        (ref.at[pl.ds(k * outs, outs), :], ref.at[pl.ds(size * outs + k, 1), :])
        for k in range(size)
    ]


def scale(copies, first, steps, loads, columns, scaled, sent):
    size = loads.shape[0]
    targets = list(zip(split(scaled, size), split(sent, size)))
    for k, copy in enumerate(copies):
        at = first + k
        copy.wait()
        rows = loads[k] * columns[:, at : at + 1]
        tail = jnp.sum(columns[:, steps + at : steps + at + 1] * rows, axis=0, keepdims=True)
        for target, target_tail in targets[k]:
            target[...] = rows
            target_tail[...] = tail


def stage_kernel(
    loads_far, observed_far, observations_far, noise_far, loads, scaled, sent, columns,
    observed, observations, noise, turned, sems, small_sems,
):
    small = [
        copied(source, target, small_sems.at[i])
        for i, (source, target) in enumerate(
            (
                (observed_far, observed),
                (observations_far, observations),
                (noise_far, noise),
            )
        )
    ]
    copies = fetched(loads_far, 0, loads, sems)
    turned[...] = jnp.zeros_like(turned)
    for copy in small:
        copy.wait()
    steps = observed.shape[0]
    root = jnp.sqrt(observed[...].astype(F32) * noise[...])
    turned[:steps, :] = root
    turned[steps : 2 * steps, :] = root * observations[...]
    columns[:, : turned.shape[0]] = turned[...].T
    scale(copies, 0, steps, loads, columns, scaled, sent)


def transition(rates, pairs, width):
    layout = pairs[...]
    rate = jnp.zeros(layout.shape, F32)
    for latent in range(rates.shape[1]):
        rate = jnp.where(layout == latent, rates[:, latent : latent + 1], rate)
    spread = lax.broadcasted_iota(jnp.int32, (layout.shape[1], width), 1) // 2
    spread = spread == lax.broadcasted_iota(jnp.int32, spread.shape, 0)
    rate = jnp.dot(
        jnp.broadcast_to(rate, (8, layout.shape[1])),
        spread.astype(F32),
        precision=lax.Precision.HIGHEST,
        preferred_element_type=F32,
    )
    even = lax.broadcasted_iota(jnp.int32, rate.shape, 1) % 2 == 0
    damping = jnp.exp(-rate)
    diagonal = jnp.where(even, damping * (1.0 + rate), damping * (1.0 - rate))
    cross = jnp.where(even, damping, -damping * rate * rate)
    return diagonal, cross


def gain_limit(block, steps):
    return min(GAIN_STEPS[block], steps) if block < len(GAIN_STEPS) else steps


def early_limit(block, size):
    return min(EARLY_STEPS[min(block, len(EARLY_STEPS) - 1)], size)


def by_block(work, steps):
    block = lax.axis_index("tm")
    kinds = min(len(GAIN_STEPS), lax.axis_size("tm") - 1)
    for i in range(1, kinds + 1):

        @pl.when(block == i if i < kinds else block >= i)
        def _():
            work(i, gain_limit(i, steps))


def fill_gains(limit, first, size, scaled, gain_high, gain_low, gained, begin=0):
    sources, targets = split(scaled, size), split(gained, size)
    end = min(size, limit - first)
    for k in range(begin, end):
        rows = sources[k][0][...]
        outs = rows.shape[0]
        if k == begin:
            tails = scaled[scaled.shape[0] - 8 :, :]
            rows = jnp.concatenate([rows, tails, tails], axis=0)
        rows = times_gain(rows, gain_high[...], gain_low[...])
        targets[k][0][...] = rows[:outs]
        if k == begin:
            for j in range(begin, end):
                targets[j][1][...] = rows[outs + j : outs + j + 1]


def rest_kernel(
    firsts, steps, loads_far, columns, rates, pairs, blend, mean,
    parts, gain_high, gain_low, initial, *rest,
):
    count = len(firsts)
    groups = [rest[3 * i : 3 * i + 3] for i in range(count)]
    sems = rest[3 * count :]
    copies = [
        fetched(loads_far, first, group[0], sem)
        for first, group, sem in zip(firsts, groups, sems)
    ]
    diagonal, cross = transition(rates, pairs, blend.shape[1])
    parts[0] = diagonal
    parts[1] = cross
    initial[...] = jnp.broadcast_to(mean[...], initial.shape)

    @pl.when(lax.axis_index("tm") != 0)
    def _():
        gain = blend[...]
        gain = gain * diagonal[0:1] + swap_pairs(gain) * cross[0:1]
        gain_high[...], gain_low[...] = halves(gain)

    for first, group, copy in zip(firsts, groups, copies):
        loads, scaled, sent = group
        scale(copy, first, steps, loads, columns, scaled, sent)


def gain_kernel(firsts, sizes, steps, gain_high, gain_low, *rest):
    count = len(firsts)

    def work(block, limit):
        for first, size, scaled, gained in zip(firsts, sizes, rest[:count], rest[count:]):
            fill_gains(limit, first, size, scaled, gain_high, gain_low, gained)

    by_block(work, steps)


def reflected(state, pull, blend):
    pull = jnp.broadcast_to(pull, state.shape)
    place = lax.broadcasted_iota(jnp.int32, (8, 128), 1) - lax.broadcasted_iota(
        jnp.int32, (8, 128), 0
    )
    turned = []
    for start in range(0, state.shape[1], 128):
        totals = [jnp.zeros((8, 128), F32) for _ in range(2)]
        for row in range(0, 128, 8):
            blended = blend[start + row : start + row + 8, :] * pull
            i = row // 8 % len(totals)
            totals[i] = totals[i] + jnp.where(
                place == row, jnp.sum(blended, axis=1, keepdims=True), 0.0
            )
        turned.append(jnp.sum(sum(totals[1:], totals[0]), axis=0, keepdims=True))
    return state - jnp.concatenate(turned, axis=1)


def advance(state, scaled, gained, parts, blend=None, beside=None):
    sides = []
    for (rows, _), (gains, _) in zip(scaled, gained):
        totals = [jnp.zeros_like(state), jnp.zeros_like(state)]
        for row in range(0, rows.shape[0], 8):
            block = rows[row : row + 8, :]
            reading = jnp.sum(block * state, axis=1, keepdims=True)
            if blend is None:
                block = gains[row : row + 8, :]
            totals[row // 8 % 2] = totals[row // 8 % 2] + reading * block
            if beside is not None and not sides:
                beside(row)
        sides.append(totals[0] + totals[1])
    pull = jnp.sum(sides[0] + sides[1], axis=0, keepdims=True)
    pull = pull - (gained[0][1][...] + gained[1][1][...])
    if blend is not None:
        state, pull = reflected(state, pull, blend), 0.0
    return state * parts[0] + swap_pairs(state) * parts[1] - pull


def part_kernel(
    early, size, steps, entering, arrived, scaled_own, parts, blend, gain_high, gain_low,
    scaled, states, leaving, *rest,
):
    *gained, sem = rest
    block = lax.axis_index("tm")

    @pl.when(block == 0)
    def _():
        state = jnp.broadcast_to(entering[0:1, :], parts.shape[1:])
        for k, pair in enumerate(zip(split(scaled_own, size), split(arrived, size))):
            state = advance(state, pair, pair, parts, blend)
            states[k : k + 1, :] = state[0:1, :]
        leaving[...] = state

    @pl.when(block != 0)
    def _():
        copied(arrived, scaled, sem).wait()

    def work(block, limit):
        limit = early_limit(block, size)
        fill_gains(limit, 0, size, arrived, gain_high, gain_low, *gained)

    if early:
        by_block(work, steps)


def late_kernel(firsts, sizes, steps, _, gain_high, gain_low, *rest):
    count = len(firsts)
    parts = list(zip(firsts, sizes, rest[:count], rest[count:]))

    def work(block, limit):
        for i, (first, size, scaled, gained) in enumerate(parts):
            begin = 0 if i else early_limit(block, size)
            fill_gains(limit, first, size, scaled, gain_high, gain_low, gained, begin)

    by_block(work, steps)


def chain(turn, entering, parts, blend, operands, early, states, observe=None):
    limit = gain_limit(turn, states.shape[0])
    state = jnp.broadcast_to(entering[0:1, :], parts.shape[1:])
    at = 0
    for loads, *refs in operands:
        size = loads.shape[0]
        early_gains = split(early, size) if at == 0 else []
        for k, (own, gained_own, other, gained) in enumerate(
            zip(*[split(ref, size) for ref in refs])
        ):
            pair = (own, other)
            beside = None
            if observe is not None and at > 0:
                beside = functools.partial(observe, at - 1, state)
            if at < limit:
                if at < early_limit(turn, len(early_gains)):
                    gained = early_gains[k]
                state = advance(state, pair, (gained_own, gained), parts, beside=beside)
            else:
                state = advance(state, pair, pair, parts, blend, beside)
            states[at : at + 1, :] = state[0:1, :]
            at += 1
    if observe is not None:
        for row in range(0, operands[0][0].shape[1], 8):
            observe(at - 1, state, row)
    return state


def grouped(refs, count):
    return [refs[5 * i : 5 * i + 5] for i in range(count)], refs[5 * count :]


def block_kernel(turn, count, before, entering, parts, blend, early, *refs):
    operands, (states, leaving) = grouped(refs, count)
    block = lax.axis_index("tm")

    @pl.when(block == turn)
    def _():
        leaving[...] = chain(turn, entering, parts, blend, operands, early, states)

    @pl.when(block != turn)
    def _():
        states[...] = before[...]
        leaving[...] = jnp.zeros_like(leaving)


def observation(operands, predicted):
    rows = [loads.at[k] for loads, *_ in operands for k in range(loads.shape[0])]
    place = lax.broadcasted_iota(jnp.int32, (8, 128), 1) - lax.broadcasted_iota(
        jnp.int32, (8, 128), 0
    )
    outs = predicted.shape[1]
    totals = {}

    def observe(at, state, row):
        reading = jnp.sum(rows[at][row : row + 8, :] * state, axis=1, keepdims=True)
        kept_rows = jnp.where(place == row % 128, reading, 0.0)
        key = (at, row // 128)
        totals[key] = totals[key] + kept_rows if key in totals else kept_rows
        if row == outs - 8:
            for start in range(0, outs, 128):
                total = jnp.sum(totals[(at, start // 128)], axis=0, keepdims=True)
                predicted[at : at + 1, start : start + 128] = total

    return observe


def own_share(states, share):
    start = pl.multiple_of(lax.axis_index("state") * share, share)
    return states[:, pl.ds(start, share)]


def finished_kernel(turn, count, states, *refs):
    loads, (own_states, predicted) = refs[:count], refs[count:]

    @pl.when(lax.axis_index("tm") != turn)
    def _():
        observe = observation([(load,) for load in loads], predicted)
        for at in range(states.shape[0]):
            state = jnp.broadcast_to(states[at : at + 1, :], (8, states.shape[1]))
            for row in range(0, loads[0].shape[1], 8):
                observe(at, state, row)
        own_states[...] = own_share(states, own_states.shape[1])


def last_kernel(turn, count, ready_states, ready, entering, parts, blend, early, *refs):
    operands, rest = grouped(refs, count)
    own_far, predicted_far, own_states, predicted, states, sems = rest

    @pl.when(lax.axis_index("tm") == turn)
    def _():
        observe = observation(operands, predicted)
        chain(turn, entering, parts, blend, operands, early, states, observe)
        own_states[...] = own_share(states, own_states.shape[1])
        first = copied(own_states, own_far, sems.at[0])
        second = copied(predicted, predicted_far, sems.at[1])
        first.wait()
        second.wait()


def hop_pairs(turn, blocks):
    if 1 < turn < blocks - 1:
        return [(i, (i + 1) % blocks) for i in range(blocks)]
    rest = [i for i in range(blocks) if i not in (turn - 1, turn)]
    pairs = [(turn - 1, turn), (turn, turn - 1)]
    for i, j in zip(rest[::2], rest[1::2]):
        pairs += [(i, j), (j, i)]
    return pairs + [(i, i) for i in rest[len(rest) // 2 * 2 :]]


def per_device(
    observations, observed, loadings, noise_precision, blend_matrix, latent_rates, pair_latent,
    initial_mean,
):
    steps, outs, width = loadings.shape
    blocks = lax.axis_size("tm")
    share = width // lax.axis_size("state")
    other = functools.partial(lax.ppermute, axis_name="outputs", perm=[(0, 1), (1, 0)])
    in_hbm = functools.partial(
        pltpu.with_memory_space_constraint, memory_space=pltpu.HBM
    )
    loadings = in_hbm(loadings)
    sizes = part_sizes(steps)
    count = len(sizes)
    firsts = [sum(sizes[:i]) for i in range(count)]

    half = 2 * 3 * outs * width * width
    vector, gain_type = kept(8, width), kept(width, width, dtype=BF16)
    sems = pltpu.SemaphoreType.DMA

    def matrices(size):
        return kept(size * outs + 8, width)

    def chunk(size):
        return [kept(size, outs, width), matrices(size), matrices(size)]

    small = (steps, outs)
    *first_chunk, columns = call(
        stage_kernel,
        "stage",
        chunk(sizes[0]) + [kept(outs, 128)],
        [FAR] * 4,
        [
            pltpu.VMEM(small, observed.dtype),
            pltpu.VMEM(small, F32),
            pltpu.VMEM((1, outs), F32),
            pltpu.VMEM((-(-2 * steps // 8) * 8, outs), F32),
            sems((sizes[0],)),
            sems((3,)),
        ],
        moved=8 * sizes[0] * outs * width,
    )(loadings, in_hbm(observed), in_hbm(observations), in_hbm(noise_precision[None, :]))
    parts, gain_high, gain_low, initial, *later = call(
        functools.partial(rest_kernel, firsts[1:], steps),
        "rest",
        [kept(2, 8, width), gain_type, gain_type, vector]
        + sum([chunk(size) for size in sizes[1:]], []),
        [FAR] + [WHOLE] * 5,
        [sems((size,)) for size in sizes[1:]],
        moved=8 * sum(sizes[1:]) * outs * width,
    )(
        loadings, columns, latent_rates[None, :], pair_latent[None, :], blend_matrix,
        initial_mean[None, :],
    )
    chunks = [first_chunk] + [later[i : i + 3] for i in range(0, len(later), 3)]
    loads_own, scaled_own, sent = zip(*chunks)
    gained_own = call(
        functools.partial(gain_kernel, firsts, sizes, steps),
        "own_gains",
        [matrices(size) for size in sizes],
        [WHOLE] * (2 + count),
        flops=steps * half,
    )(gain_high, gain_low, *scaled_own)

    leaving = initial
    scaled, states, early = [], [], []
    for i in range(count):
        rows, state, leaving, *gained = call(
            functools.partial(part_kernel, i == 0, sizes[i], steps),
            "other_part",
            [matrices(sizes[i]), kept(sizes[i], width), vector]
            + ([matrices(sizes[i])] if i == 0 else []),
            [WHOLE] * 7,
            [sems],
            flops=sizes[i] * half // 3,
            moved=8 * sizes[i] * outs * width,
        )(
            leaving, other(sent[i]), scaled_own[i], parts, blend_matrix, gain_high, gain_low
        )
        scaled.append(rows)
        states.append(state)
        early += gained
    states = jnp.concatenate(states, axis=0)
    gained = call(
        functools.partial(late_kernel, firsts, sizes, steps),
        "late_gains",
        [matrices(size) for size in sizes],
        [FAR] + [WHOLE] * (2 + count),
        flops=steps * half,
    )(leaving, gain_high, gain_low, *scaled)
    operands = [*early]
    for group in zip(loads_own, scaled_own, gained_own, scaled, gained):
        operands += group

    specs = [WHOLE] * (4 + len(operands))
    entering = leaving
    for turn in range(1, blocks):
        entering = lax.ppermute(leaving, "tm", hop_pairs(turn, blocks))
        if turn < blocks - 1:
            states, leaving = call(
                functools.partial(block_kernel, turn, count),
                "block_chain",
                [kept(steps, width), vector],
                specs,
                flops=steps * half,
            )(states, entering, parts, blend_matrix, *operands)
    last = blocks - 1 if blocks > 1 else -1
    outputs = [
        jax.ShapeDtypeStruct((steps, share), F32),
        jax.ShapeDtypeStruct((steps, outs), F32),
    ]
    ready = call(
        functools.partial(finished_kernel, last, count),
        "finished",
        outputs,
        [WHOLE] * (1 + count),
        flops=steps * half,
    )(states, *loads_own)
    return tuple(
        call(
            functools.partial(last_kernel, last, count),
            "last_chain",
            outputs,
            [FAR] * 2 + [WHOLE] * (3 + len(operands)),
            [
                pltpu.VMEM((steps, share), F32),
                pltpu.VMEM((steps, outs), F32),
                pltpu.VMEM((steps, width), F32),
                sems((2,)),
            ],
            flops=steps * half,
            out_spec=FAR,
            aliases=((0, 0), (1, 1)),
        )(*ready, entering, parts, blend_matrix, *operands)
    )


def solution(mesh):
    placed = (
        P("tm", "outputs"),
        P("tm", "outputs"),
        P("tm", "outputs", None),
        P("outputs"),
        P(),
        P(),
        P(),
        P(),
    )
    return jax.shard_map(
        per_device,
        mesh=mesh,
        in_specs=placed,
        out_specs=(P("tm", "state"), P("tm", "outputs")),
        check_vma=False,
    )
```

```python
import functools

import jax
import jax.numpy as jnp
from jax import lax
from jax.experimental import pallas as pl
from jax.experimental.pallas import tpu as pltpu
from jax.sharding import PartitionSpec as P

F32, BF16 = jnp.float32, jnp.bfloat16
VMEM_LIMIT = 8 * 2**20
LAST_PART = 1
PARTS = 4
GAIN_STEPS = (0, 9, 10)
EARLY_STEPS = (0, 4, 3, 0)
WHOLE = pl.BlockSpec(memory_space=pltpu.VMEM)
FAR = pl.BlockSpec(memory_space=pl.ANY)


def call(kernel, name, outs, in_specs, scratch=(), flops=0, moved=0, out_spec=WHOLE, aliases=()):
    return pl.pallas_call(
        kernel,
        out_shape=outs,
        in_specs=in_specs,
        out_specs=[out_spec] * len(outs),
        input_output_aliases=dict(aliases),
        scratch_shapes=scratch,
        compiler_params=pltpu.CompilerParams(vmem_limit_bytes=VMEM_LIMIT),
        cost_estimate=pl.CostEstimate(flops=flops, bytes_accessed=moved, transcendentals=0),
        name=name,
    )


def kept(*shape, dtype=F32):
    return pltpu.VMEM(shape, dtype)


def swap_pairs(x):
    width = x.shape[-1]
    lane = lax.broadcasted_iota(jnp.int32, x.shape, 1)
    return jnp.where(lane % 2 == 0, pltpu.roll(x, width - 1, 1), pltpu.roll(x, 1, 1))


def halves(x):
    high = x.astype(BF16)
    return high, (x - high.astype(F32)).astype(BF16)


def times_gain(scaled, gain_high, gain_low):
    high, low = halves(scaled)
    dot = functools.partial(jnp.dot, preferred_element_type=F32)
    return dot(high, gain_high) + (dot(high, gain_low) + dot(low, gain_high))


def part_sizes(steps):
    rest = steps - LAST_PART
    sizes = [(rest + PARTS - 2 - i) // (PARTS - 1) for i in range(PARTS - 1)]
    return sizes + [LAST_PART]


def copied(source, target, sem):
    copy = pltpu.make_async_copy(source, target, sem)
    copy.start()
    return copy


def fetched(loads_far, first, loads, sems):
    return [
        copied(loads_far.at[first + k], loads.at[k], sems.at[k]) for k in range(loads.shape[0])
    ]


def split(ref, size):
    outs = (ref.shape[0] - 8) // size
    return [
        (ref.at[pl.ds(k * outs, outs), :], ref.at[pl.ds(size * outs + k, 1), :])
        for k in range(size)
    ]


def scale(copies, first, steps, loads, columns, scaled, sent):
    size = loads.shape[0]
    targets = list(zip(split(scaled, size), split(sent, size)))
    for k, copy in enumerate(copies):
        at = first + k
        copy.wait()
        rows = loads[k] * columns[:, at : at + 1]
        tail = jnp.sum(columns[:, steps + at : steps + at + 1] * rows, axis=0, keepdims=True)
        for target, target_tail in targets[k]:
            target[...] = rows
            target_tail[...] = tail


def stage_kernel(
    loads_far, observed_far, observations_far, noise_far, loads, scaled, sent, columns,
    observed, observations, noise, turned, sems, small_sems,
):
    small = [
        copied(source, target, small_sems.at[i])
        for i, (source, target) in enumerate(
            (
                (observed_far, observed),
                (observations_far, observations),
                (noise_far, noise),
            )
        )
    ]
    copies = fetched(loads_far, 0, loads, sems)
    turned[...] = jnp.zeros_like(turned)
    for copy in small:
        copy.wait()
    steps = observed.shape[0]
    root = jnp.sqrt(observed[...].astype(F32) * noise[...])
    turned[:steps, :] = root
    turned[steps : 2 * steps, :] = root * observations[...]
    columns[:, : turned.shape[0]] = turned[...].T
    scale(copies, 0, steps, loads, columns, scaled, sent)


def transition(rates, pairs, width):
    layout = pairs[...]
    rate = jnp.zeros(layout.shape, F32)
    for latent in range(rates.shape[1]):
        rate = jnp.where(layout == latent, rates[:, latent : latent + 1], rate)
    spread = lax.broadcasted_iota(jnp.int32, (layout.shape[1], width), 1) // 2
    spread = spread == lax.broadcasted_iota(jnp.int32, spread.shape, 0)
    rate = jnp.dot(
        jnp.broadcast_to(rate, (8, layout.shape[1])),
        spread.astype(F32),
        precision=lax.Precision.HIGHEST,
        preferred_element_type=F32,
    )
    even = lax.broadcasted_iota(jnp.int32, rate.shape, 1) % 2 == 0
    damping = jnp.exp(-rate)
    diagonal = jnp.where(even, damping * (1.0 + rate), damping * (1.0 - rate))
    cross = jnp.where(even, damping, -damping * rate * rate)
    return diagonal, cross


def gain_limit(block, steps):
    return min(GAIN_STEPS[block], steps) if block < len(GAIN_STEPS) else steps


def early_limit(block, size):
    return min(EARLY_STEPS[min(block, len(EARLY_STEPS) - 1)], size)


def by_block(work, steps):
    block = lax.axis_index("tm")
    kinds = min(len(GAIN_STEPS), lax.axis_size("tm") - 1)
    for i in range(1, kinds + 1):

        @pl.when(block == i if i < kinds else block >= i)
        def _():
            work(i, gain_limit(i, steps))


def fill_gains(limit, first, size, scaled, gain_high, gain_low, gained, begin=0):
    sources, targets = split(scaled, size), split(gained, size)
    end = min(size, limit - first)
    for k in range(begin, end):
        rows = sources[k][0][...]
        outs = rows.shape[0]
        if k == begin:
            tails = scaled[scaled.shape[0] - 8 :, :]
            rows = jnp.concatenate([rows, tails, tails], axis=0)
        rows = times_gain(rows, gain_high[...], gain_low[...])
        targets[k][0][...] = rows[:outs]
        if k == begin:
            for j in range(begin, end):
                targets[j][1][...] = rows[outs + j : outs + j + 1]


def rest_kernel(
    firsts, steps, loads_far, columns, rates, pairs, blend, mean,
    parts, gain_high, gain_low, initial, *rest,
):
    count = len(firsts)
    groups = [rest[3 * i : 3 * i + 3] for i in range(count)]
    sems = rest[3 * count :]
    copies = [
        fetched(loads_far, first, group[0], sem)
        for first, group, sem in zip(firsts, groups, sems)
    ]
    diagonal, cross = transition(rates, pairs, blend.shape[1])
    parts[0] = diagonal
    parts[1] = cross
    initial[...] = jnp.broadcast_to(mean[...], initial.shape)

    @pl.when(lax.axis_index("tm") != 0)
    def _():
        gain = blend[...]
        gain = gain * diagonal[0:1] + swap_pairs(gain) * cross[0:1]
        gain_high[...], gain_low[...] = halves(gain)

    for first, group, copy in zip(firsts, groups, copies):
        loads, scaled, sent = group
        scale(copy, first, steps, loads, columns, scaled, sent)


def gain_kernel(firsts, sizes, steps, gain_high, gain_low, *rest):
    count = len(firsts)

    def work(block, limit):
        for first, size, scaled, gained in zip(firsts, sizes, rest[:count], rest[count:]):
            fill_gains(limit, first, size, scaled, gain_high, gain_low, gained)

    by_block(work, steps)


def reflected(state, pull, blend):
    pull = jnp.broadcast_to(pull, state.shape)
    place = lax.broadcasted_iota(jnp.int32, (8, 128), 1) - lax.broadcasted_iota(
        jnp.int32, (8, 128), 0
    )
    turned = []
    for start in range(0, state.shape[1], 128):
        totals = [jnp.zeros((8, 128), F32) for _ in range(2)]
        for row in range(0, 128, 8):
            blended = blend[start + row : start + row + 8, :] * pull
            i = row // 8 % len(totals)
            totals[i] = totals[i] + jnp.where(
                place == row, jnp.sum(blended, axis=1, keepdims=True), 0.0
            )
        turned.append(jnp.sum(sum(totals[1:], totals[0]), axis=0, keepdims=True))
    return state - jnp.concatenate(turned, axis=1)


def advance(state, scaled, gained, parts, blend=None, beside=None):
    sides = []
    for (rows, _), (gains, _) in zip(scaled, gained):
        totals = [jnp.zeros_like(state), jnp.zeros_like(state)]
        for row in range(0, rows.shape[0], 8):
            block = rows[row : row + 8, :]
            reading = jnp.sum(block * state, axis=1, keepdims=True)
            if blend is None:
                block = gains[row : row + 8, :]
            totals[row // 8 % 2] = totals[row // 8 % 2] + reading * block
            if beside is not None and not sides:
                beside(row)
        sides.append(totals[0] + totals[1])
    pull = jnp.sum(sides[0] + sides[1], axis=0, keepdims=True)
    pull = pull - (gained[0][1][...] + gained[1][1][...])
    if blend is not None:
        state, pull = reflected(state, pull, blend), 0.0
    return state * parts[0] + swap_pairs(state) * parts[1] - pull


def part_kernel(
    early, size, steps, entering, arrived, scaled_own, parts, blend, gain_high, gain_low,
    scaled, states, leaving, *rest,
):
    *gained, sem = rest
    block = lax.axis_index("tm")

    @pl.when(block == 0)
    def _():
        state = jnp.broadcast_to(entering[0:1, :], parts.shape[1:])
        for k, pair in enumerate(zip(split(scaled_own, size), split(arrived, size))):
            state = advance(state, pair, pair, parts, blend)
            states[k : k + 1, :] = state[0:1, :]
        leaving[...] = state

    @pl.when(block != 0)
    def _():
        copied(arrived, scaled, sem).wait()

    def work(block, limit):
        limit = early_limit(block, size)
        fill_gains(limit, 0, size, arrived, gain_high, gain_low, *gained)

    if early:
        by_block(work, steps)


def late_kernel(firsts, sizes, steps, _, gain_high, gain_low, *rest):
    count = len(firsts)
    parts = list(zip(firsts, sizes, rest[:count], rest[count:]))

    def work(block, limit):
        for i, (first, size, scaled, gained) in enumerate(parts):
            begin = 0 if i else early_limit(block, size)
            fill_gains(limit, first, size, scaled, gain_high, gain_low, gained, begin)

    by_block(work, steps)


def chain(turn, entering, parts, blend, operands, early, states, observe=None):
    limit = gain_limit(turn, states.shape[0])
    state = jnp.broadcast_to(entering[0:1, :], parts.shape[1:])
    at = 0
    for loads, *refs in operands:
        size = loads.shape[0]
        early_gains = split(early, size) if at == 0 else []
        for k, (own, gained_own, other, gained) in enumerate(
            zip(*[split(ref, size) for ref in refs])
        ):
            pair = (own, other)
            beside = None
            if observe is not None and at > 0:
                beside = functools.partial(observe, at - 1, state)
            if at < limit:
                if at < early_limit(turn, len(early_gains)):
                    gained = early_gains[k]
                state = advance(state, pair, (gained_own, gained), parts, beside=beside)
            else:
                state = advance(state, pair, pair, parts, blend, beside)
            states[at : at + 1, :] = state[0:1, :]
            at += 1
    if observe is not None:
        for row in range(0, operands[0][0].shape[1], 8):
            observe(at - 1, state, row)
    return state


def grouped(refs, count):
    return [refs[5 * i : 5 * i + 5] for i in range(count)], refs[5 * count :]


def block_kernel(turn, count, before, entering, parts, blend, early, *refs):
    operands, (states, leaving) = grouped(refs, count)
    block = lax.axis_index("tm")

    @pl.when(block == turn)
    def _():
        leaving[...] = chain(turn, entering, parts, blend, operands, early, states)

    @pl.when(block != turn)
    def _():
        states[...] = before[...]
        leaving[...] = jnp.zeros_like(leaving)


def observation(operands, predicted):
    rows = [loads.at[k] for loads, *_ in operands for k in range(loads.shape[0])]
    place = lax.broadcasted_iota(jnp.int32, (8, 128), 1) - lax.broadcasted_iota(
        jnp.int32, (8, 128), 0
    )
    outs = predicted.shape[1]
    totals = {}

    def observe(at, state, row):
        reading = jnp.sum(rows[at][row : row + 8, :] * state, axis=1, keepdims=True)
        kept_rows = jnp.where(place == row % 128, reading, 0.0)
        key = (at, row // 128)
        totals[key] = totals[key] + kept_rows if key in totals else kept_rows
        if row == outs - 8:
            for start in range(0, outs, 128):
                total = jnp.sum(totals[(at, start // 128)], axis=0, keepdims=True)
                predicted[at : at + 1, start : start + 128] = total

    return observe


def own_share(states, share):
    start = pl.multiple_of(lax.axis_index("state") * share, share)
    return states[:, pl.ds(start, share)]


def finished_kernel(turn, count, states, *refs):
    loads, (own_states, predicted) = refs[:count], refs[count:]

    @pl.when(lax.axis_index("tm") != turn)
    def _():
        observe = observation([(load,) for load in loads], predicted)
        for at in range(states.shape[0]):
            state = jnp.broadcast_to(states[at : at + 1, :], (8, states.shape[1]))
            for row in range(0, loads[0].shape[1], 8):
                observe(at, state, row)
        own_states[...] = own_share(states, own_states.shape[1])


def last_kernel(turn, count, ready_states, ready, entering, parts, blend, early, *refs):
    operands, rest = grouped(refs, count)
    own_far, predicted_far, own_states, predicted, states, sems = rest

    @pl.when(lax.axis_index("tm") == turn)
    def _():
        observe = observation(operands, predicted)
        chain(turn, entering, parts, blend, operands, early, states, observe)
        own_states[...] = own_share(states, own_states.shape[1])
        first = copied(own_states, own_far, sems.at[0])
        second = copied(predicted, predicted_far, sems.at[1])
        first.wait()
        second.wait()


def hop_pairs(turn, blocks):
    if 1 < turn < blocks - 1:
        return [(i, (i + 1) % blocks) for i in range(blocks)]
    rest = [i for i in range(blocks) if i not in (turn - 1, turn)]
    pairs = [(turn - 1, turn), (turn, turn - 1)]
    for i, j in zip(rest[::2], rest[1::2]):
        pairs += [(i, j), (j, i)]
    return pairs + [(i, i) for i in rest[len(rest) // 2 * 2 :]]


def per_device(
    observations, observed, loadings, noise_precision, blend_matrix, latent_rates, pair_latent,
    initial_mean,
):
    steps, outs, width = loadings.shape
    blocks = lax.axis_size("tm")
    share = width // lax.axis_size("state")
    other = functools.partial(lax.ppermute, axis_name="outputs", perm=[(0, 1), (1, 0)])
    in_hbm = functools.partial(
        pltpu.with_memory_space_constraint, memory_space=pltpu.HBM
    )
    loadings = in_hbm(loadings)
    sizes = part_sizes(steps)
    count = len(sizes)
    firsts = [sum(sizes[:i]) for i in range(count)]

    half = 2 * 3 * outs * width * width
    vector, gain_type = kept(8, width), kept(width, width, dtype=BF16)
    sems = pltpu.SemaphoreType.DMA

    def matrices(size):
        return kept(size * outs + 8, width)

    def chunk(size):
        return [kept(size, outs, width), matrices(size), matrices(size)]

    small = (steps, outs)
    *first_chunk, columns = call(
        stage_kernel,
        "stage",
        chunk(sizes[0]) + [kept(outs, 128)],
        [FAR] * 4,
        [
            pltpu.VMEM(small, observed.dtype),
            pltpu.VMEM(small, F32),
            pltpu.VMEM((1, outs), F32),
            pltpu.VMEM((-(-2 * steps // 8) * 8, outs), F32),
            sems((sizes[0],)),
            sems((3,)),
        ],
        moved=8 * sizes[0] * outs * width,
    )(loadings, in_hbm(observed), in_hbm(observations), in_hbm(noise_precision[None, :]))
    parts, gain_high, gain_low, initial, *later = call(
        functools.partial(rest_kernel, firsts[1:], steps),
        "rest",
        [kept(2, 8, width), gain_type, gain_type, vector]
        + sum([chunk(size) for size in sizes[1:]], []),
        [FAR] + [WHOLE] * 5,
        [sems((size,)) for size in sizes[1:]],
        moved=8 * sum(sizes[1:]) * outs * width,
    )(
        loadings, columns, latent_rates[None, :], pair_latent[None, :], blend_matrix,
        initial_mean[None, :],
    )
    chunks = [first_chunk] + [later[i : i + 3] for i in range(0, len(later), 3)]
    loads_own, scaled_own, sent = zip(*chunks)
    gained_own = call(
        functools.partial(gain_kernel, firsts, sizes, steps),
        "own_gains",
        [matrices(size) for size in sizes],
        [WHOLE] * (2 + count),
        flops=steps * half,
    )(gain_high, gain_low, *scaled_own)

    leaving = initial
    scaled, states, early = [], [], []
    for i in range(count):
        rows, state, leaving, *gained = call(
            functools.partial(part_kernel, i == 0, sizes[i], steps),
            "other_part",
            [matrices(sizes[i]), kept(sizes[i], width), vector]
            + ([matrices(sizes[i])] if i == 0 else []),
            [WHOLE] * 7,
            [sems],
            flops=sizes[i] * half // 3,
            moved=8 * sizes[i] * outs * width,
        )(
            leaving, other(sent[i]), scaled_own[i], parts, blend_matrix, gain_high, gain_low
        )
        scaled.append(rows)
        states.append(state)
        early += gained
    states = jnp.concatenate(states, axis=0)
    gained = call(
        functools.partial(late_kernel, firsts, sizes, steps),
        "late_gains",
        [matrices(size) for size in sizes],
        [FAR] + [WHOLE] * (2 + count),
        flops=steps * half,
    )(leaving, gain_high, gain_low, *scaled)
    operands = [*early]
    for group in zip(loads_own, scaled_own, gained_own, scaled, gained):
        operands += group

    specs = [WHOLE] * (4 + len(operands))
    entering = leaving
    for turn in range(1, blocks):
        entering = lax.ppermute(leaving, "tm", hop_pairs(turn, blocks))
        if turn < blocks - 1:
            states, leaving = call(
                functools.partial(block_kernel, turn, count),
                "block_chain",
                [kept(steps, width), vector],
                specs,
                flops=steps * half,
            )(states, entering, parts, blend_matrix, *operands)
    last = blocks - 1 if blocks > 1 else -1
    outputs = [
        jax.ShapeDtypeStruct((steps, share), F32),
        jax.ShapeDtypeStruct((steps, outs), F32),
    ]
    ready = call(
        functools.partial(finished_kernel, last, count),
        "finished",
        outputs,
        [WHOLE] * (1 + count),
        flops=steps * half,
    )(states, *loads_own)
    return tuple(
        call(
            functools.partial(last_kernel, last, count),
            "last_chain",
            outputs,
            [FAR] * 2 + [WHOLE] * (3 + len(operands)),
            [
                pltpu.VMEM((steps, share), F32),
                pltpu.VMEM((steps, outs), F32),
                pltpu.VMEM((steps, width), F32),
                sems((2,)),
            ],
            flops=steps * half,
            out_spec=FAR,
            aliases=((0, 0), (1, 1)),
        )(*ready, entering, parts, blend_matrix, *operands)
    )


def solution(mesh):
    placed = (
        P("tm", "outputs"),
        P("tm", "outputs"),
        P("tm", "outputs", None),
        P("outputs"),
        P(),
        P(),
        P(),
        P(),
    )
    return jax.shard_map(
        per_device,
        mesh=mesh,
        in_specs=placed,
        out_specs=(P("tm", "state"), P("tm", "outputs")),
        check_vma=False,
    )
```
